256 devices in a mesh: grp: 2 (over x_lo), mp: 128 (over x_hi, y, z, core).
Axes of the slice: x: 4 (x_hi: 2, x_lo: 2; x = x_hi * 2 + x_lo), y: 4, z: 8, core: 2. Of those that a mesh axis runs over, the one named last changes fastest.
Arguments:
- latents: bfloat16 [8, 1024, 64], P(None, ('grp', 'mp')), may hold values from -6 to 6
- noise: bfloat16 [8, 1024, 64], P(None, ('grp', 'mp')), may hold values from -6 to 6
- steps_t: int32 [8], replicated, may hold values from 20 to 979
- w_in: bfloat16 [2, 64, 3072], P('grp'), may hold values from -0.75 to 0.75
- norm_gain: float32 [2, 3072], P('grp'), may hold values from 0.5 to 1.5
- w_qkv: bfloat16 [2, 16, 3072, 384], P('grp', None, 'mp'), may hold values from -0.109375 to 0.109375
- q_gain: float32 [2, 16, 128], P('grp'), may hold values from 0.25 to 1.75
- k_gain: float32 [2, 16, 128], P('grp'), may hold values from 0.25 to 1.75
- w_out: bfloat16 [2, 2048, 64], P('grp'), may hold values from -0.125 to 0.125
Outputs:
- gen_grad: float32 [8, 1024, 64], P(None, ('grp', 'mp'))
- fake_grad: float32 [16, 3072, 384], P(None, ('grp', 'mp'))
The draws below stay inside these ranges and needn't reach their ends.
All inputs are finite; a program needn't handle non-finite values.
Results may differ from the reference program's by a relative error of at most 0.0075.
Values may be sent and summed in bfloat16 or wider, within the bound.
A program may use at most 128 MiB of HBM per device.

```python
import math
import jax
import jax.numpy as jnp
from jax import lax

D = 3072
HD = 128
CH = 64
HEADS_WIN = 16
LEN = 1024
SAMPLES = 8


def touch_ends(result, stream_key, least, largest):
    spot = [jax.random.randint(jax.random.fold_in(stream_key, axis), (), 0, length) for axis, length in enumerate(result.shape)]
    widest = result.shape.index(max(result.shape))
    beside = spot[:widest] + [(spot[widest] + 1) % result.shape[widest]] + spot[widest + 1:]
    return result.at[tuple(spot)].set(least).at[tuple(beside)].set(largest)


def block_scale(own_key, shape, split, smallest, high):
    loudness, own = 1.0, jax.random.fold_in(own_key, 6)
    for dim, parts in split:
        draws = jnp.exp(jax.random.uniform(jax.random.fold_in(own, dim), (parts,), jnp.float32, smallest / len(split), high / len(split)))
        loudness = loudness * jnp.repeat(draws, shape[dim] // parts).reshape([-1 if axis == dim else 1 for axis in range(len(shape))])
    return loudness


def scatter_about(own_key, dims, spread, bound, split=(), kind=jnp.bfloat16):
    drawn = spread * jax.random.normal(own_key, dims, jnp.float32)
    if split:
        drawn = drawn * block_scale(own_key, dims, split, -0.22, 0.18)
    return jnp.clip(drawn, -bound, bound).astype(kind)


def setup_inputs(seed: int = 0) -> dict:
    seeds = jax.random.split(jax.random.key(seed), 10)
    return {
        "latents": scatter_about(seeds[0], (SAMPLES, LEN, CH), 1.0, 6.0, ((1, 256),)),
        "noise": scatter_about(seeds[1], (SAMPLES, LEN, CH), 1.0, 6.0, ((1, 256),)),
        "steps_t": touch_ends(jax.random.randint(seeds[2], (SAMPLES,), 20, 980), jax.random.fold_in(seeds[2], 1), 20, 979).astype(jnp.int32),
        "w_in": scatter_about(seeds[3], (2, CH, D), CH ** -0.5, 0.75, ((0, 2),)),
        "norm_gain": jnp.clip(1.0 + 0.1 * jax.random.normal(seeds[4], (2, D), jnp.float32), 0.5, 1.5),
        "w_qkv": scatter_about(seeds[5], (2, HEADS_WIN, D, 3 * HD), D ** -0.5, 0.109375, ((0, 2), (2, 128))),
        "q_gain": jnp.clip(1.0 + 0.15 * jax.random.normal(seeds[6], (2, HEADS_WIN, HD), jnp.float32), 0.25, 1.75),
        "k_gain": jnp.clip(1.0 + 0.15 * jax.random.normal(seeds[7], (2, HEADS_WIN, HD), jnp.float32), 0.25, 1.75),
        "w_out": scatter_about(seeds[8], (2, HEADS_WIN * HD, CH), (HEADS_WIN * HD) ** -0.5, 0.125, ((0, 2),)),
    }


def time_embed(t_value, width):
    half = width // 2
    index = jnp.arange(half).astype(jnp.float32)
    freqs = jnp.exp(-math.log(10000.0) * index / half)
    phase = t_value * freqs
    return jnp.concatenate([jnp.sin(phase), jnp.cos(phase)])

def embed_tokens(noisy_rows, weight_in, gain, temb_row):
    x_val = jnp.dot(noisy_rows, weight_in, preferred_element_type=jnp.float32) + temb_row
    scaled = x_val * lax.rsqrt(lax.optimization_barrier(jnp.mean(x_val * x_val, axis=-1, keepdims=True)) + 1e-06) * gain
    return scaled.astype(jnp.bfloat16)

def head_forward(qkv, gain_q, gain_k, out_rows):
    width = gain_q.shape[0]
    query = qkv[:, :width]
    keyed = qkv[:, width:2 * width]
    value = qkv[:, 2 * width:]
    q_norm = (query * lax.rsqrt(lax.optimization_barrier(jnp.mean(query * query, axis=-1, keepdims=True)) + 1e-06) * gain_q).astype(jnp.bfloat16)
    k_norm = (keyed * lax.rsqrt(lax.optimization_barrier(jnp.mean(keyed * keyed, axis=-1, keepdims=True)) + 1e-06) * gain_k).astype(jnp.bfloat16)
    scores = lax.dot_general(q_norm, k_norm, (((1,), (1,)), ((), ())), preferred_element_type=jnp.float32) * (1.0 / math.sqrt(width))
    expo = jnp.exp(scores)
    probs = (expo / lax.optimization_barrier(jnp.sum(expo, axis=-1, keepdims=True))).astype(jnp.bfloat16)
    attended = jnp.dot(probs, value.astype(jnp.bfloat16), preferred_element_type=jnp.float32).astype(jnp.bfloat16)
    return jnp.dot(attended, out_rows, preferred_element_type=jnp.float32)

def reference(latents, noise, steps_t, w_in, norm_gain, w_qkv, q_gain, k_gain, w_out):
    t_float = steps_t.astype(jnp.float32)
    angle = 0.5 * math.pi / 1000.0 * t_float
    alpha = jnp.cos(angle)[:, None, None]
    sigma = jnp.sin(angle)[:, None, None]
    noisy = (alpha * latents.astype(jnp.float32) + sigma * noise.astype(jnp.float32)).astype(jnp.bfloat16)
    temb = jax.vmap(lambda tv: time_embed(tv, D))(t_float)
    head_size = q_gain.shape[2]

    def head_qkv(xn_rows, net, head):
        return jnp.dot(xn_rows, w_qkv[net, head], preferred_element_type=jnp.float32)

    def out_rows(net, head):
        return lax.dynamic_slice_in_dim(w_out[net], head * head_size, head_size, 0)

    def predict(net):

        def one_sample(pair):
            noisy_rows, temb_row = pair
            xn_rows = embed_tokens(noisy_rows, w_in[net], norm_gain[net], temb_row)

            def one_head(head):
                qkv = head_qkv(xn_rows, net, head)
                return head_forward(qkv, q_gain[net, head], k_gain[net, head], out_rows(net, head))
            return lax.optimization_barrier(jnp.sum(lax.map(one_head, jnp.arange(HEADS_WIN)), axis=0))
        return lax.map(one_sample, (noisy, temb))
    pred_real = predict(0)
    pred_fake = predict(1)
    gen_grad = pred_fake - pred_real
    dpred = (pred_fake - latents.astype(jnp.float32)) / SAMPLES

    def grad_step(total, triple):
        noisy_rows, temb_row, cot_rows = triple
        xn_rows = embed_tokens(noisy_rows, w_in[1], norm_gain[1], temb_row)

        def one_head(head):
            qkv = head_qkv(xn_rows, 1, head)
            gq = q_gain[1, head]
            gk = k_gain[1, head]
            orow = out_rows(1, head)
            unused, pullback = jax.vjp(lambda qv: head_forward(qv, gq, gk, orow), qkv)
            dqkv = pullback(cot_rows)[0].astype(jnp.bfloat16)
            term = lax.dot_general(xn_rows, dqkv, (((0,), (0,)), ((), ())), preferred_element_type=jnp.float32)
            return term.astype(jnp.bfloat16)
        terms = lax.map(one_head, jnp.arange(HEADS_WIN))
        return (total + terms.astype(jnp.float32), None)
    start = jnp.zeros((HEADS_WIN, D, 3 * head_size), jnp.float32)
    fake_grad, unused_out = lax.scan(grad_step, start, (noisy, temb, dpred))
    return (gen_grad, fake_grad)
```

```python
import functools
import math

import jax
import jax.numpy as jnp
from jax import lax
from jax.experimental import pallas as pl
from jax.experimental.pallas import tpu as pltpu
from jax.sharding import PartitionSpec as P

MESH = pl.DeviceIdType.MESH
XH, NY, NZ, NC = 2, 4, 8, 2
HEADS, SAMPLES = XH * NZ, NY * NC
D, HD, CH, LEN = 3072, 128, 64, 1024
TRIPLE = 3 * HD
BF, F32 = jnp.bfloat16, jnp.float32


def place():
    m = lax.axis_index("mp")
    return (
        lax.axis_index("grp"),
        m // (NY * NZ * NC),
        (m // (NZ * NC)) % NY,
        (m // NC) % NZ,
        m % NC,
    )


def device(g, xh, y, z, c):
    return (g, ((xh * NY + y) * NZ + z) * NC + c)


def rows(start, size, step):
    return pl.ds(pl.multiple_of(start, step), size)


def send(src, dst, ssem, rsem, target):
    copy = pltpu.make_async_remote_copy(
        src_ref=src, dst_ref=dst, send_sem=ssem, recv_sem=rsem, device_id=target, device_id_type=MESH
    )
    copy.start()


def take(ref, sem):
    pltpu.make_async_copy(ref, ref, sem).wait()


def greet(barrier, target):
    pl.semaphore_signal(barrier, inc=1, device_id=target, device_id_type=MESH)


Z_ORDER = (0, 1, 7, 2, 6, 3, 5, 4)


def gather_kernel(
    w_ref, nl_ref, W, NL, w0s, w0r, w1s, n1r, n1f,
    n1_s, n1_r, nz_s, nz_r, nx_s, nx_r, w0_s, w0_r, w_s, w1_r, wa_r, wb_r, wr_r, sb_r,
):
    g, xh, y, z, c = place()
    cross = xh != c
    X = xh * 2 + g
    barrier = pltpu.get_barrier_semaphore()
    for dy in range(NY):
        for dc in range(NC):
            if dy or dc:
                greet(barrier, device(g, xh, (y + dy) % NY, z, (c + dc) % NC))
    for dz in range(1, NZ):
        greet(barrier, device(g, xh, y, (z + dz) % NZ, c))
    for dx in range(1, 4):
        X2 = (X + dx) % 4
        greet(barrier, device(X2 % 2, X2 // 2, y, z, c))

    @pl.when(cross)
    def _():
        for dz in range(NZ):
            greet(barrier, device(g, c, y, (z + dz) % NZ, xh))

    pl.semaphore_wait(barrier, 7 + 7 + 3 + jnp.where(cross, NZ, 0))

    me_b = y * NC + c
    for dy in range(NY):
        for dc in range(NC):
            y2, c2 = (y + dy) % NY, (c + dc) % NC
            b2 = y2 * NC + c2
            if dy or dc:
                send(nl_ref.at[b2], n1r.at[me_b], n1_s, n1_r, device(g, xh, y2, z, c2))
            else:
                pltpu.make_async_copy(nl_ref.at[b2], n1r.at[me_b], n1_r).start()

    for j in range(NZ):
        w0s[j, 0:24, :] = w_ref[(1 - c) * NZ + j]
        w0s[j, 24:32, :] = jnp.zeros((8, TRIPLE), BF)
    send(w0s, w0r, w0_s, w0_r, device(g, xh, y, z, 1 - c))

    take(n1r, n1_r)
    for j in range(SAMPLES):
        n1f[j * 4 : j * 4 + 4, :] = n1r[j, 0:4, :].astype(F32)
    own_n = rows((X * NZ + z) * 32, 32, 32)
    NL[own_n, :] = n1f[...].astype(BF)
    for dz in Z_ORDER[1:]:
        send(NL.at[own_n], NL.at[own_n], nz_s, nz_r, device(g, xh, y, (z + dz) % NZ, c))

    take(w0r, w0_r)
    for j in range(NZ):
        mine = w_ref[c * NZ + j].astype(F32)
        theirs = w0r[j, 0:24, :].astype(F32)
        low = jnp.where(c == 0, mine, theirs)
        high = jnp.where(c == 0, theirs, mine)
        w1s[j] = jnp.concatenate([low, high], axis=0).astype(BF)
    for dz in Z_ORDER:
        z2 = (z + dz) % NZ
        src, dst = w1s.at[z2], W.at[rows(((xh * NY + y) * NZ + z) * 48, 48, 48)]
        if dz:
            send(src, dst, w_s, w1_r.at[dz], device(g, c, y, z2, xh))
        else:

            @pl.when(cross)
            def _():
                send(src, dst, w_s, w1_r.at[dz], device(g, c, y, z2, xh))

            @pl.when(jnp.logical_not(cross))
            def _():
                pltpu.make_async_copy(src, dst, w1_r.at[dz]).start()

    take(NL.at[0 : 7 * 32], nz_r)
    own_x = rows(X * 256, 256, 256)
    for dx in range(1, 4):
        X2 = (X + dx) % 4
        send(NL.at[own_x], NL.at[own_x], nx_s, nx_r, device(X2 % 2, X2 // 2, y, z, c))

    up, down = device(g, xh, (y + 1) % NY, z, c), device(g, xh, (y + 3) % NY, z, c)
    sib = device(g, xh, y, z, 1 - c)

    def piece(dy, dz):
        return W.at[rows(((c * NY + (y + dy) % NY) * NZ + (z + 8 - dz) % NZ) * 48, 48, 48)]

    def pass_on(ref, rsem, target):
        send(ref, ref, w_s, rsem, target)

    for s in range(NZ + 4):
        if s < NZ:
            dz = Z_ORDER[s]
            ref = piece(0, dz)
            take(ref, w1_r.at[dz])
            pass_on(ref, wa_r.at[dz], up)
            pass_on(ref, wb_r.at[dz], down)
            pass_on(ref, sb_r, sib)
        if 2 <= s < NZ + 2:
            dz = Z_ORDER[s - 2]
            ref = piece(3, dz)
            take(ref, wa_r.at[dz])
            if s % 2 == 0:
                pass_on(ref, wr_r.at[dz], up)
            pass_on(ref, sb_r, sib)
            ref = piece(1, dz)
            take(ref, wb_r.at[dz])
            if s % 2 == 1:
                pass_on(ref, wr_r.at[dz], down)
            pass_on(ref, sb_r, sib)
        if s >= 4:
            dz = Z_ORDER[s - 4]
            ref = piece(2, dz)
            take(ref, wr_r.at[dz])
            pass_on(ref, sb_r, sib)

    take(W.at[0 : D // 2], sb_r)
    take(NL.at[0 : 3 * 256], nx_r)
    take(n1r.at[0:7], n1_s)
    take(w0s, w0_s)
    take(NL.at[0 : 7 * 32], nz_s)
    take(NL.at[0 : 3 * 256], nx_s)
    take(W.at[0 : 63 * 48], w_s)

    @pl.when(cross)
    def _():
        take(W.at[0:48], w_s)


DMA = pltpu.SemaphoreType.DMA
VM = pl.BlockSpec(memory_space=pltpu.VMEM)


def params(cid):
    return pltpu.CompilerParams(
        collective_id=cid, has_side_effects=True, vmem_limit_bytes=48 * 1024 * 1024
    )


def gather(w_local, nl_send):
    return pl.pallas_call(
        gather_kernel,
        out_shape=(jax.ShapeDtypeStruct((D, TRIPLE), BF), jax.ShapeDtypeStruct((LEN, 128), BF)),
        in_specs=[VM, VM],
        out_specs=(VM, VM),
        scratch_shapes=[
            pltpu.VMEM((NZ, 32, TRIPLE), BF),
            pltpu.VMEM((NZ, 32, TRIPLE), BF),
            pltpu.VMEM((NZ, 48, TRIPLE), BF),
            pltpu.VMEM((SAMPLES, 16, 128), BF),
            pltpu.VMEM((32, 128), F32),
            DMA, DMA, DMA, DMA, DMA, DMA, DMA, DMA, DMA,
            DMA((NZ,)), DMA((NZ,)), DMA((NZ,)), DMA((NZ,)), DMA,
        ],
        compiler_params=params(0),
        name="gather",
    )(w_local, nl_send)


def pred_kernel(
    pp, lat, gen, cot, p1r, dch, pmine, pother, gs, p1_s, p1_r, d_s, d_r, x_s, x_r, g_s, g_r
):
    g, xh, y, z, c = place()
    h, me_b = xh * NZ + z, y * NC + c
    barrier = pltpu.get_barrier_semaphore()
    for dh in range(1, HEADS):
        h2 = (h + dh) % HEADS
        greet(barrier, device(g, h2 // NZ, y, h2 % NZ, c))
    for dy in range(NY):
        for dc in range(NC):
            if dy or dc:
                greet(barrier, device(g, xh, (y + dy) % NY, z, (c + dc) % NC))
    greet(barrier, device(1 - g, xh, y, z, c))
    pl.semaphore_wait(barrier, 15 + 7 + 1)

    for dh in range(1, HEADS):
        h2 = (h + dh) % HEADS
        send(pp.at[rows(h2 * 32, 32, 32)], p1r.at[h], p1_s, p1_r, device(g, h2 // NZ, y, h2 % NZ, c))
    pltpu.make_async_copy(pp.at[rows(h * 32, 32, 32)], p1r.at[h], p1_r).start()
    take(p1r, p1_r)
    pred = jnp.sum(p1r[...].astype(F32), axis=0)
    pmine[...] = pred
    partner = device(1 - g, xh, y, z, c)
    send(pmine, pother, x_s, x_r, partner)

    @pl.when(g == 1)
    def _():
        dch[...] = ((pred - lat[...].astype(F32)) * (1.0 / SAMPLES)).astype(BF)
        own = rows(h * 32, 32, 32)
        for dh in range(1, HEADS):
            h2 = (h + dh) % HEADS
            send(dch, cot.at[own], d_s, d_r, device(g, h2 // NZ, y, h2 % NZ, c))
        pltpu.make_async_copy(dch, cot.at[own], d_r).start()

    take(pother, x_r)
    diff = jnp.where(g == 0, pother[...] - pmine[...], pmine[...] - pother[...])
    low = diff[:, 0:CH]
    high = diff[:, CH:]
    mine = jnp.where(g == 0, low, high)
    for j in range(SAMPLES):
        gs[j, 0:4, 0:CH] = mine[j * 4 : j * 4 + 4, :]
    for dy in range(NY):
        for dc in range(NC):
            y2, c2 = (y + dy) % NY, (c + dc) % NC
            b2 = y2 * NC + c2
            if dy or dc:
                send(gs.at[b2], gen.at[me_b], g_s, g_r, device(g, xh, y2, z, c2))
            else:
                pltpu.make_async_copy(gs.at[b2], gen.at[me_b], g_r).start()
    take(gen, g_r)
    take(pmine, x_s)
    take(gs.at[0:7], g_s)
    take(p1r.at[0:15], p1_s)

    @pl.when(g == 1)
    def _():
        take(cot, d_r)
        take(p1r.at[0:15], d_s)


def reduce_pred(pp, lat):
    return pl.pallas_call(
        pred_kernel,
        out_shape=(
            jax.ShapeDtypeStruct((SAMPLES, 8, 128), F32),
            jax.ShapeDtypeStruct((LEN // 2, 128), BF),
        ),
        in_specs=[VM, VM],
        out_specs=(VM, VM),
        scratch_shapes=[
            pltpu.VMEM((HEADS, 32, 128), BF),
            pltpu.VMEM((32, 128), BF),
            pltpu.VMEM((32, 128), F32),
            pltpu.VMEM((32, 128), F32),
            pltpu.VMEM((SAMPLES, 8, 128), F32),
            DMA, DMA, DMA, DMA, DMA, DMA, DMA, DMA,
        ],
        compiler_params=params(1),
        name="reduce_pred",
    )(pp, lat)


HALF, PART = D // 2, 192


def scatter_kernel(
    term, R, sibr, rel_s, rel_r, st, yst, yr, fin, sb_s, sb_r, rl_s, rl_r, y_s, y_r, f_s, f_r
):
    g, xh, y, z, c = place()
    h = xh * NZ + z
    barrier = pltpu.get_barrier_semaphore()
    fake = g == 1

    def is_me(xh2, z2, c2):
        return (xh2 == xh) & (z2 == z) & (c2 == c) & fake

    def targets():
        for dx in range(XH):
            for dz in Z_ORDER:
                for dc in range(NC):
                    yield (xh + dx) % XH, (z + dz) % NZ, (c + dc) % NC

    for dx in range(XH):
        for dz in range(NZ):
            xh2, z2 = (xh + dx) % XH, (z + dz) % NZ

            @pl.when(jnp.logical_not(is_me(xh2, z2, g)))
            def _():
                greet(barrier, device(1, xh2, y, z2, g))

    @pl.when(fake)
    def _():
        up, down = device(1, xh, (y + 1) % NY, z, c), device(1, xh, (y + 3) % NY, z, c)
        sib = device(1, xh, y, z, 1 - c)
        for t in (up, down, sib):
            greet(barrier, t)
        pl.semaphore_wait(barrier, 3 + 32 - c)

        def part(j, x2):
            return (x2 * NY + (y + j) % NY) * PART

        for j in (2, 1, 3, 0):
            for x2 in range(XH):
                src = term.at[rows((1 - c) * HALF + part(j, x2), PART, 16)]
                send(src, sibr.at[rows(part(j, x2), PART, 16)], sb_s, sb_r.at[j], sib)

        def local(j, x2):
            mine = term[rows(c * HALF + part(j, x2), PART, 16), :].astype(F32)
            return mine + sibr[rows(part(j, x2), PART, 16), :].astype(F32)

        take(sibr.at[0 : 2 * PART], sb_r.at[2])
        for x2, t in ((0, up), (1, down)):
            rel_s[x2] = local(2, x2).astype(BF)
            send(rel_s.at[x2], rel_r.at[x2], rl_s, rl_r.at[x2], t)
        for j, x2, t in ((1, 1, up), (3, 0, down)):
            take(sibr.at[0 : 2 * PART], sb_r.at[j])
            yst[j // 2, x2] = local(j, x2).astype(BF)
            send(yst.at[j // 2, x2], yr.at[j // 2, x2], y_s, y_r, t)
        for j, x2, t in ((1, 0, up), (3, 1, down)):
            take(rel_r.at[x2], rl_r.at[x2])
            yst[j // 2, x2] = (local(j, x2) + rel_r[x2].astype(F32)).astype(BF)
            send(yst.at[j // 2, x2], yr.at[j // 2, x2], y_s, y_r, t)
        take(sibr.at[0 : 2 * PART], sb_r.at[0])
        for x2 in range(XH):
            fin[x2] = local(0, x2)
        take(yr, y_r)
        for x2 in range(XH):
            fin[x2] = fin[x2] + yr[0, x2].astype(F32) + yr[1, x2].astype(F32)
        for x2 in range(XH):
            for z2 in range(NZ):
                for c2 in range(NC):
                    i = z2 * NC + c2
                    st[(x2 * NZ + z2) * NC + c2, 0:12, :] = fin[x2, i * 12 : i * 12 + 12, :].astype(BF)
        for xh2, z2, c2 in targets():
            src = st.at[(xh2 * NZ + z2) * NC + c2]
            me = (xh2 == xh) & (z2 == z) & (c2 == c) & (c == 1)

            @pl.when(me)
            def _():
                pltpu.make_async_copy(src, R.at[h], f_r).start()

            @pl.when(jnp.logical_not(me))
            def _():
                send(src, R.at[h], f_s, f_r, device(c, xh2, y, z2, c2))

        take(sibr, sb_s)
        take(rel_s, rl_s)
        take(yst, y_s)
        take(st.at[0:31], f_s)

        @pl.when(c == 0)
        def _():
            take(st.at[0], f_s)

    take(R, f_r)


def scatter_grad(term):
    return pl.pallas_call(
        scatter_kernel,
        out_shape=jax.ShapeDtypeStruct((HEADS, 16, TRIPLE), BF),
        in_specs=[VM],
        out_specs=VM,
        scratch_shapes=[
            pltpu.VMEM((HALF, TRIPLE), BF),
            pltpu.VMEM((XH, PART, TRIPLE), BF),
            pltpu.VMEM((XH, PART, TRIPLE), BF),
            pltpu.VMEM((32, 16, TRIPLE), BF),
            pltpu.VMEM((2, XH, PART, TRIPLE), BF),
            pltpu.VMEM((2, XH, PART, TRIPLE), BF),
            pltpu.VMEM((XH, PART, TRIPLE), F32),
            DMA, DMA((NY,)), DMA, DMA((XH,)), DMA, DMA, DMA, DMA,
        ],
        compiler_params=params(2),
        name="scatter_grad",
    )(term)


def time_embed(t_value, width):
    half = width // 2
    index = jnp.arange(half).astype(jnp.float32)
    freqs = jnp.exp(-math.log(10000.0) * index / half)
    phase = t_value * freqs
    return jnp.concatenate([jnp.sin(phase), jnp.cos(phase)])


def embed_tokens(noisy_rows, weight_in, gain, temb_row):
    x_val = jnp.dot(noisy_rows, weight_in, preferred_element_type=jnp.float32) + temb_row
    scaled = x_val * lax.rsqrt(jnp.mean(x_val * x_val, axis=-1, keepdims=True) + 1e-06) * gain
    return scaled.astype(jnp.bfloat16)


def head_forward(qkv, gain_q, gain_k, out_rows):
    width = gain_q.shape[0]
    query = qkv[:, :width]
    keyed = qkv[:, width : 2 * width]
    value = qkv[:, 2 * width :]
    q_norm = (
        query * lax.rsqrt(jnp.mean(query * query, axis=-1, keepdims=True) + 1e-06) * gain_q
    ).astype(jnp.bfloat16)
    k_norm = (
        keyed * lax.rsqrt(jnp.mean(keyed * keyed, axis=-1, keepdims=True) + 1e-06) * gain_k
    ).astype(jnp.bfloat16)
    scores = lax.dot_general(
        q_norm, k_norm, (((1,), (1,)), ((), ())), preferred_element_type=jnp.float32
    ) * (1.0 / math.sqrt(width))
    expo = jnp.exp(scores)
    probs = (expo / jnp.sum(expo, axis=-1, keepdims=True)).astype(jnp.bfloat16)
    attended = jnp.dot(
        probs, value.astype(jnp.bfloat16), preferred_element_type=jnp.float32
    ).astype(jnp.bfloat16)
    return jnp.dot(attended, out_rows, preferred_element_type=jnp.float32)


def on_device(latents, noise, steps_t, w_in, norm_gain, w_qkv, q_gain, k_gain, w_out):
    g, xh, y, z, c = place()
    head, sample = xh * NZ + z, y * NC + c
    t_float = steps_t.astype(F32)
    angle = 0.5 * math.pi / 1000.0 * t_float
    alpha = jnp.cos(angle)[:, None, None]
    sigma = jnp.sin(angle)[:, None, None]
    noisy = (alpha * latents.astype(F32) + sigma * noise.astype(F32)).astype(BF)
    nl_send = jnp.pad(jnp.concatenate([noisy, latents], axis=-1), ((0, 0), (0, 12), (0, 0)))
    w_head, nl = gather(w_qkv[0], nl_send)
    temb_row = time_embed(lax.dynamic_index_in_dim(t_float, sample, 0, keepdims=False), D)
    xn_rows = embed_tokens(nl[:, :CH], w_in[0], norm_gain[0], temb_row)
    qkv = jnp.dot(xn_rows, w_head, preferred_element_type=F32)
    gain_q = lax.dynamic_index_in_dim(q_gain[0], head, 0, keepdims=False)
    gain_k = lax.dynamic_index_in_dim(k_gain[0], head, 0, keepdims=False)
    out_rows = lax.dynamic_slice_in_dim(w_out[0], head * HD, HD, 0)
    partial_pred, pullback = jax.vjp(lambda qv: head_forward(qv, gain_q, gain_k, out_rows), qkv)
    pp = partial_pred.astype(BF).reshape(XH, 2, 256, CH).transpose(0, 2, 1, 3).reshape(512, 128)
    lat = nl[:, CH:].reshape(XH, 2, 256, CH).transpose(0, 2, 1, 3).reshape(512, 128)
    lat = lax.dynamic_slice_in_dim(lat, head * 32, 32, 0)
    gen, cot = reduce_pred(pp, lat)
    gen_grad = gen[:, :4, :CH]

    def fake_terms():
        cot_rows = cot.reshape(XH, 256, 2, CH).transpose(0, 2, 1, 3).reshape(LEN, CH).astype(F32)
        dqkv = pullback(cot_rows)[0].astype(BF)
        term = lax.dot_general(xn_rows, dqkv, (((0,), (0,)), ((), ())), preferred_element_type=F32)
        return term.astype(BF)

    def real_terms():
        return jnp.zeros((D, TRIPLE), BF)

    term = lax.cond(g == 1, fake_terms, real_terms)
    fake_grad = scatter_grad(term)[:, :12, :].astype(F32)
    return gen_grad, fake_grad


def solution(mesh):
    return jax.shard_map(
        on_device,
        mesh=mesh,
        in_specs=(
            P(None, ("grp", "mp"), None),
            P(None, ("grp", "mp"), None),
            P(),
            P("grp", None, None),
            P("grp", None),
            P("grp", None, "mp", None),
            P("grp", None, None),
            P("grp", None, None),
            P("grp", None, None),
        ),
        out_specs=(P(None, ("grp", "mp"), None), P(None, ("grp", "mp"), None)),
        check_vma=False,
    )
```

```python
import functools
import math

import jax
import jax.numpy as jnp
from jax import lax
from jax.experimental import pallas as pl
from jax.experimental.pallas import tpu as pltpu
from jax.sharding import PartitionSpec as P

MESH = pl.DeviceIdType.MESH
XH, NY, NZ, NC = 2, 4, 8, 2
HEADS, SAMPLES = XH * NZ, NY * NC
D, HD, CH, LEN = 3072, 128, 64, 1024
TRIPLE = 3 * HD
BF, F32 = jnp.bfloat16, jnp.float32


def place():
    m = lax.axis_index("mp")
    return (
        lax.axis_index("grp"),
        m // (NY * NZ * NC),
        (m // (NZ * NC)) % NY,
        (m // NC) % NZ,
        m % NC,
    )


def device(g, xh, y, z, c):
    return (g, ((xh * NY + y) * NZ + z) * NC + c)


def mod(a, n):
    return lax.rem(a, n)


def rows(start, size, step):
    return pl.ds(pl.multiple_of(start, step), size)


def send(src, dst, ssem, rsem, target):
    copy = pltpu.make_async_remote_copy(
        src_ref=src, dst_ref=dst, send_sem=ssem, recv_sem=rsem, device_id=target, device_id_type=MESH
    )
    copy.start()


def take(ref, sem):
    pltpu.make_async_copy(ref, ref, sem).wait()


def greet(barrier, target):
    pl.semaphore_signal(barrier, inc=1, device_id=target, device_id_type=MESH)


Z_ORDER = (0, 1, 7, 2, 6, 3, 5, 4)


DMA = pltpu.SemaphoreType.DMA
VM = pl.BlockSpec(memory_space=pltpu.VMEM)
SM = pl.BlockSpec(memory_space=pltpu.SMEM)
HALF, PART, QUART = D // 2, 192, 96
TILE = 256
SCALE = 1.0 / math.sqrt(HD)


def dot(a, b, ca=1, cb=0):
    return lax.dot_general(a, b, (((ca,), (cb,)), ((), ())), preferred_element_type=F32)


SCRATCH = dict(
    W=((D, TRIPLE), BF),
    NL=((LEN, 128), BF),
    w0s=((NZ, 32, TRIPLE), BF),
    w0r=((NZ, 32, TRIPLE), BF),
    w1s=((NZ, 48, TRIPLE), BF),
    nst=((SAMPLES, 16, 128), BF),
    n1r=((SAMPLES, 16, 128), BF),
    nsf=((SAMPLES, 16, 128), F32),
    n1f=((32, 128), F32),
    temb=((8, D), F32),
    xf=((128, D), F32),
    xn=((LEN, D), BF),
    xnT=((D, LEN), BF),
    qkv=((LEN, TRIPLE), F32),
    qn=((LEN, HD), BF),
    kn=((LEN, HD), BF),
    v=((LEN, HD), BF),
    knT=((HD, LEN), BF),
    vT=((HD, LEN), BF),
    p32=((4, LEN, TILE), F32),
    pb=((4, LEN, TILE), BF),
    pp=((LEN // 2, 128), BF),
    p1r=((HEADS, 32, 128), BF),
    dch=((32, 128), BF),
    cot=((LEN // 2, 128), BF),
    pmine=((32, 128), F32),
    pother=((32, 128), F32),
    gs=((SAMPLES, 8, 128), F32),
    dq=((LEN, HD), F32),
    dk=((LEN, HD), F32),
    dv=((LEN, HD), F32),
    dqkv=((LEN, TRIPLE), BF),
    T=((D, TRIPLE), BF),
    sibr=((HALF, TRIPLE), BF),
    rel_s=((XH, 2, QUART, TRIPLE), BF),
    rel_r=((XH, 2, QUART, TRIPLE), BF),
    yst=((2, XH, PART, TRIPLE), BF),
    yr=((2, XH, PART, TRIPLE), BF),
    fin=((XH, PART, TRIPLE), F32),
    st=((32, 16, TRIPLE), BF),
)
SEMS = dict(
    n1_s=None, n1_r=None, nz_s=None, nz_r=None, nx_s=None, nx_r=None, w0_s=None, w0_r=None, w_s=None,
    w1_r=NZ, wa_r=NZ, wb_r=NZ, wr_r=NZ, sb_r=None, p1_s=None, p1_r=None, d_s=None, d_r=None,
    x_s=None, x_r=None, g_s=None, g_r=None, ts_s=None, ts_r=NY, rl_s=None, rl_r=(XH, 2), y_s=None,
    y_r=XH, f_s=None, f_r=None,
)
INPUTS = ("lat", "noise", "steps", "w_in", "gain", "w_qkv", "q_gain", "k_gain", "w_out")


class Refs:
    pass


def mega_kernel(*args):
    r = Refs()
    names = INPUTS + ("gen", "R") + tuple(SCRATCH) + tuple(SEMS)
    for name, ref in zip(names, args, strict=True):
        setattr(r, name, ref)
    g, xh, y, z, c = place()
    h, me_b, X = xh * NZ + z, y * NC + c, xh * 2 + g
    fake, cross = g == 1, xh != c
    W, NL = r.W, r.NL

    def yc(dy, dc):
        return mod(y + dy, NY), mod(c + dc, NC)

    def zline(dz):
        return device(g, xh, y, mod(z + dz, NZ), c)

    def xline(dx):
        X2 = mod(X + dx, 4)
        return device(mod(X2, 2), X2 // 2, y, z, c)

    barrier = pltpu.get_barrier_semaphore()
    for dy in range(NY):
        for dc in range(NC):
            if dy or dc:
                y2, c2 = yc(dy, dc)
                greet(barrier, device(g, xh, y2, z, c2))
    for dz in range(1, NZ):
        greet(barrier, zline(dz))
    for dx in range(1, 4):
        greet(barrier, xline(dx))

    @pl.when(cross)
    def _():
        for dz in range(NZ):
            greet(barrier, device(g, c, y, mod(z + dz, NZ), xh))

    for j in range(NZ):
        r.w0s[j, 0:24, :] = r.w_qkv[0, (1 - c) * NZ + j]
        r.w0s[j, 24:32, :] = jnp.zeros((8, TRIPLE), BF)

    rows8 = lax.broadcasted_iota(jnp.int32, (SAMPLES, 128), 0)
    ang = jnp.zeros((SAMPLES, 128), F32)
    for b in range(SAMPLES):
        ang = jnp.where(rows8 == b, r.steps[b].astype(F32), ang)
    ang = 0.5 * math.pi / 1000.0 * ang
    alpha, sigma = jnp.cos(ang), jnp.sin(ang)
    r.nsf[...] = jnp.zeros_like(r.nsf)
    for b in range(SAMPLES):
        latent = r.lat[b].astype(F32)
        noisy = alpha[b : b + 1, 0:CH] * latent + sigma[b : b + 1, 0:CH] * r.noise[b].astype(F32)
        r.nsf[b, 0:4, 0:CH] = noisy
        r.nsf[b, 0:4, CH:128] = latent
    r.nst[...] = r.nsf[...].astype(BF)

    pl.semaphore_wait(barrier, 7 + 7 + 3 + jnp.where(cross, NZ, 0))

    sib = device(g, xh, y, z, 1 - c)
    send(r.w0s, r.w0r, r.w0_s, r.w0_r, sib)
    for dy in range(NY):
        for dc in range(NC):
            y2, c2 = yc(dy, dc)
            src = r.nst.at[y2 * NC + c2]
            if dy or dc:
                send(src, r.n1r.at[me_b], r.n1_s, r.n1_r, device(g, xh, y2, z, c2))
            else:
                pltpu.make_async_copy(src, r.n1r.at[me_b], r.n1_r).start()

    take(r.w0r, r.w0_r)
    for j in range(NZ):
        mine = r.w_qkv[0, c * NZ + j].astype(F32)
        theirs = r.w0r[j, 0:24, :].astype(F32)
        low = jnp.where(c == 0, mine, theirs)
        high = jnp.where(c == 0, theirs, mine)
        r.w1s[j] = jnp.concatenate([low, high], axis=0).astype(BF)
    for dz in Z_ORDER:
        z2 = mod(z + dz, NZ)
        src, dst = r.w1s.at[z2], W.at[rows(((xh * NY + y) * NZ + z) * 48, 48, 48)]
        if dz:
            send(src, dst, r.w_s, r.w1_r.at[dz], device(g, c, y, z2, xh))
        else:

            @pl.when(cross)
            def _():
                send(src, dst, r.w_s, r.w1_r.at[dz], device(g, c, y, z2, xh))

            @pl.when(jnp.logical_not(cross))
            def _():
                pltpu.make_async_copy(src, dst, r.w1_r.at[dz]).start()

    take(r.n1r, r.n1_r)
    for j in range(SAMPLES):
        r.n1f[j * 4 : j * 4 + 4, :] = r.n1r[j, 0:4, :].astype(F32)
    own_n = rows((X * NZ + z) * 32, 32, 32)
    NL[own_n, :] = r.n1f[...].astype(BF)
    for dz in Z_ORDER[1:]:
        send(NL.at[own_n], NL.at[own_n], r.nz_s, r.nz_r, zline(dz))

    up, down = device(g, xh, mod(y + 1, NY), z, c), device(g, xh, mod(y + 3, NY), z, c)

    def piece(dy, dz):
        return W.at[rows(((c * NY + mod(y + dy, NY)) * NZ + mod(z + 8 - dz, NZ)) * 48, 48, 48)]

    def pass_on(ref, rsem, target):
        send(ref, ref, r.w_s, rsem, target)

    def relay(s):
        if s < NZ:
            dz = Z_ORDER[s]
            ref = piece(0, dz)
            take(ref, r.w1_r.at[dz])
            pass_on(ref, r.wa_r.at[dz], up)
            pass_on(ref, r.wb_r.at[dz], down)
            pass_on(ref, r.sb_r, sib)
        if 2 <= s < NZ + 2:
            dz = Z_ORDER[s - 2]
            ref = piece(3, dz)
            take(ref, r.wa_r.at[dz])
            if s % 2 == 0:
                pass_on(ref, r.wr_r.at[dz], up)
            pass_on(ref, r.sb_r, sib)
            ref = piece(1, dz)
            take(ref, r.wb_r.at[dz])
            if s % 2 == 1:
                pass_on(ref, r.wr_r.at[dz], down)
            pass_on(ref, r.sb_r, sib)
        if s >= 4:
            dz = Z_ORDER[s - 4]
            ref = piece(2, dz)
            take(ref, r.wr_r.at[dz])
            pass_on(ref, r.sb_r, sib)

    t_value = r.steps[me_b].astype(F32)
    index = lax.broadcasted_iota(jnp.int32, (1, D // 2), 1).astype(F32)
    phase = t_value * jnp.exp(-math.log(10000.0) * index / (D // 2))
    r.temb[0:1, 0 : D // 2] = jnp.sin(phase)
    r.temb[0:1, D // 2 :] = jnp.cos(phase)

    relay(0)
    relay(1)
    take(NL.at[0 : 7 * 32], r.nz_r)
    own_x = rows(X * 256, 256, 256)
    for dx in range(1, 4):
        send(NL.at[own_x], NL.at[own_x], r.nx_s, r.nx_r, xline(dx))
    relay(2)
    relay(3)

    def embed(tile):
        at = rows(tile * 128, 128, 128)
        noisy = NL[at, :][:, 0:CH]
        total = jnp.zeros((128, 128), F32)
        for k in range(D // 512):
            part = dot(noisy, r.w_in[0, :, k * 512 : k * 512 + 512]) + r.temb[0:1, k * 512 : k * 512 + 512]
            r.xf[:, k * 512 : k * 512 + 512] = part
            sq = part * part
            for i in range(4):
                total = total + sq[:, i * 128 : i * 128 + 128]
        inv = lax.rsqrt(jnp.sum(total, axis=1, keepdims=True) * (1.0 / D) + 1e-06)
        for k in range(D // 512):
            cols = slice(k * 512, k * 512 + 512)
            done = (r.xf[:, cols] * inv * r.gain[0:1, cols]).astype(BF)
            r.xn[at, cols] = done

            @pl.when(fake)
            def _():
                r.xnT[cols, at] = done.T

    embed(X * 2)
    relay(4)
    embed(X * 2 + 1)
    relay(5)
    take(NL.at[0 : 3 * 256], r.nx_r)
    for i in range(6):
        tile = mod(X * 2 + 2 + i, 8)
        embed(tile)
        relay(6 + i)

    def project(half, first):
        cols = rows(half * HALF, HALF, HALF)
        for i in range(4):
            at = slice(i * TILE, i * TILE + TILE)
            part = dot(r.xn[at, cols], W[cols, :])
            r.qkv[at, :] = part if first else r.qkv[at, :] + part

    project(c, True)
    take(W.at[0:HALF], r.sb_r)
    project(1 - c, False)

    gain_q, gain_k = r.q_gain[0, pl.ds(h, 1), :], r.k_gain[0, pl.ds(h, 1), :]

    def normed(lanes):
        raw = r.qkv[:, lanes]
        inv = lax.rsqrt(jnp.mean(raw * raw, axis=-1, keepdims=True) + 1e-06)
        return raw, inv

    q_l, k_l, v_l = slice(0, HD), slice(HD, 2 * HD), slice(2 * HD, TRIPLE)
    raw, inv = normed(q_l)
    r.qn[...] = (raw * inv * gain_q).astype(BF)
    raw, inv = normed(k_l)
    k_norm = (raw * inv * gain_k).astype(BF)
    r.kn[...] = k_norm
    r.knT[...] = k_norm.T
    value = r.qkv[:, v_l].astype(BF)
    r.v[...] = value
    r.vT[...] = value.T
    w_out = r.w_out[0, rows(h * HD, HD, HD), :]

    halves = []
    for t in range(4):
        at = slice(t * TILE, t * TILE + TILE)
        scores = dot(r.kn[...], r.qn[at, :], 1, 1)
        expo = jnp.exp2(scores * (SCALE * math.log2(math.e)))
        probs = expo * (1.0 / jnp.sum(expo, axis=0, keepdims=True))
        r.p32[t] = probs
        probs = probs.astype(BF)
        r.pb[t] = probs
        attended = dot(r.vT[...], probs).astype(BF)
        halves.append(dot(attended.T, w_out))
        if t % 2 == 1:
            x2 = t // 2
            r.pp[x2 * 256 : x2 * 256 + 256, :] = jnp.concatenate(halves, axis=1).astype(BF)
            halves = []
            for dz in Z_ORDER:
                z2 = mod(z + dz, NZ)
                src, dst = r.pp.at[rows((x2 * NZ + z2) * 32, 32, 32)], r.p1r.at[h]
                if dz:
                    send(src, dst, r.p1_s, r.p1_r, device(g, x2, y, z2, c))
                else:

                    @pl.when(xh == x2)
                    def _():
                        pltpu.make_async_copy(src, dst, r.p1_r).start()

                    @pl.when(xh != x2)
                    def _():
                        send(src, dst, r.p1_s, r.p1_r, device(g, x2, y, z2, c))

    take(r.p1r, r.p1_r)
    pred = jnp.sum(r.p1r[...].astype(F32), axis=0)
    r.pmine[...] = pred

    @pl.when(fake)
    def _():
        lat0 = NL[rows((xh * 2 * NZ + z) * 32, 32, 32), :].astype(F32)[:, CH:]
        lat1 = NL[rows(((xh * 2 + 1) * NZ + z) * 32, 32, 32), :].astype(F32)[:, CH:]
        latent = jnp.concatenate([lat0, lat1], axis=1)
        r.dch[...] = ((pred - latent) * (1.0 / SAMPLES)).astype(BF)
        own = rows(h * 32, 32, 32)
        for dx in range(XH):
            for dz in Z_ORDER:
                if dx or dz:
                    target = device(g, mod(xh + dx, XH), y, mod(z + dz, NZ), c)
                    send(r.dch, r.cot.at[own], r.d_s, r.d_r, target)
        pltpu.make_async_copy(r.dch, r.cot.at[own], r.d_r).start()

    partner = device(1 - g, xh, y, z, c)
    send(r.pmine, r.pother, r.x_s, r.x_r, partner)

    def generator():
        take(r.pother, r.x_r)
        diff = jnp.where(g == 0, r.pother[...] - r.pmine[...], r.pmine[...] - r.pother[...])
        mine = jnp.where(g == 0, diff[:, 0:CH], diff[:, CH:])
        for j in range(SAMPLES):
            r.gs[j, 0:4, 0:CH] = mine[j * 4 : j * 4 + 4, :]
        for dy in range(NY):
            for dc in range(NC):
                y2, c2 = yc(dy, dc)
                src, dst = r.gs.at[y2 * NC + c2], r.gen.at[me_b]
                if dy or dc:
                    send(src, dst, r.g_s, r.g_r, device(g, xh, y2, z, c2))
                else:
                    pltpu.make_async_copy(src, dst, r.g_r).start()

    @pl.when(jnp.logical_not(fake))
    def _():
        generator()

    @pl.when(fake)
    def _():
        take(r.cot, r.d_r)
        for t in range(4):
            at = slice(t * TILE, t * TILE + TILE)
            cot = r.cot[(t // 2) * 256 : (t // 2) * 256 + 256, (t % 2) * CH : (t % 2) * CH + CH]
            d_att = dot(cot, w_out, 1, 1).astype(BF)
            d_probs = dot(r.v[...], d_att, 1, 1)
            probs = r.p32[t]
            mean = jnp.sum(probs * d_probs, axis=0, keepdims=True)
            d_score = (probs * (d_probs - mean)).astype(BF)
            dv = dot(r.pb[t], d_att)
            dk = dot(d_score, r.qn[at, :])
            if t:
                r.dv[...] += dv
                r.dk[...] += dk
            else:
                r.dv[...] = dv
                r.dk[...] = dk
            r.dq[at, :] = dot(r.knT[...], d_score).T

        def unnorm(lanes, gain, grad):
            raw, inv = normed(lanes)
            scaled = grad * SCALE * gain
            unit = raw * inv
            inner = jnp.mean(unit * scaled, axis=-1, keepdims=True)
            return (inv * (scaled - unit * inner)).astype(BF)

        r.dqkv[:, q_l] = unnorm(q_l, gain_q, r.dq[...])
        r.dqkv[:, k_l] = unnorm(k_l, gain_k, r.dk[...])
        r.dqkv[:, v_l] = r.dv[...].astype(BF)

        def part(half, j, x2):
            return half * HALF + (x2 * NY + mod(y + j, NY)) * PART

        def block(half, j):
            at0, at1 = rows(part(half, j, 0), PART, PART), rows(part(half, j, 1), PART, PART)
            left = jnp.concatenate([r.xnT[at0, :], r.xnT[at1, :]], axis=0)
            out = dot(left, r.dqkv[...]).astype(BF)
            r.T[at0, :] = out[:PART]
            r.T[at1, :] = out[PART:]

        def to_sibling(j):
            block(1 - c, j)
            for x2 in range(XH):
                src = r.T.at[rows(part(1 - c, j, x2), PART, PART)]
                send(src, r.sibr.at[rows(part(0, j, x2), PART, PART)], r.ts_s, r.ts_r.at[j], sib)

        def arrived(j):
            take(r.sibr.at[0 : 2 * PART], r.ts_r.at[j])

        def local(j, x2, zh=None):
            if zh is None:
                off, size = 0, PART
            else:
                off, size = zh * QUART, QUART
            mine = r.T[rows(part(c, j, x2) + off, size, QUART), :].astype(F32)
            return mine + r.sibr[rows(part(0, j, x2) + off, size, QUART), :].astype(F32)

        def relay_out(x2):
            for zh, t in ((0, up), (1, down)):
                r.rel_s[x2, zh] = local(2, x2, zh).astype(BF)
                send(r.rel_s.at[x2, zh], r.rel_r.at[x2, zh], r.rl_s, r.rl_r.at[x2, zh], t)

        def plain_out(x2):
            for d, j, zh, t in ((0, 1, 1, up), (1, 3, 0, down)):
                at = slice(zh * QUART, zh * QUART + QUART)
                r.yst[d, x2, at, :] = local(j, x2, zh).astype(BF)
                send(r.yst.at[d, x2, at], r.yr.at[d, x2, at], r.y_s, r.y_r.at[x2], t)

        def joined_out(x2):
            for d, j, zh, t in ((0, 1, 0, up), (1, 3, 1, down)):
                at = slice(zh * QUART, zh * QUART + QUART)
                take(r.rel_r.at[x2, zh], r.rl_r.at[x2, zh])
                both = local(j, x2, zh) + r.rel_r[x2, zh].astype(F32)
                r.yst[d, x2, at, :] = both.astype(BF)
                send(r.yst.at[d, x2, at], r.yr.at[d, x2, at], r.y_s, r.y_r.at[x2], t)

        to_sibling(2)
        block(c, 2)
        to_sibling(1)
        to_sibling(3)
        arrived(2)
        relay_out(0)
        block(c, 1)
        block(c, 3)
        arrived(1)
        arrived(3)
        plain_out(0)
        relay_out(1)
        to_sibling(0)
        joined_out(0)
        plain_out(1)
        block(c, 0)
        joined_out(1)
        generator()
        arrived(0)
        for x2 in range(XH):
            take(r.yr.at[:, x2], r.y_r.at[x2])
            r.fin[x2] = local(0, x2) + r.yr[0, x2].astype(F32) + r.yr[1, x2].astype(F32)
            for i in range(NZ * NC):
                r.st[x2 * NZ * NC + i, 0:12, :] = r.fin[x2, i * 12 : i * 12 + 12, :].astype(BF)
            for dz in Z_ORDER:
                for c2 in range(NC):
                    z2 = mod(z + dz, NZ)
                    src = r.st.at[(x2 * NZ + z2) * NC + c2]
                    target = device(c, x2, y, z2, c2)
                    if dz or c2 == 0:
                        send(src, r.R.at[h], r.f_s, r.f_r, target)
                    else:
                        me = (xh == x2) & (c == 1)

                        @pl.when(me)
                        def _():
                            pltpu.make_async_copy(src, r.R.at[h], r.f_r).start()

                        @pl.when(jnp.logical_not(me))
                        def _():
                            send(src, r.R.at[h], r.f_s, r.f_r, target)

        take(r.cot.at[0 : 15 * 32], r.d_s)
        take(r.sibr, r.ts_s)
        take(r.rel_s, r.rl_s)
        take(r.yst, r.y_s)
        take(r.st.at[0:31], r.f_s)

        @pl.when(c == 0)
        def _():
            take(r.st.at[0], r.f_s)

    take(r.n1r.at[0:7], r.n1_s)
    take(r.w0s, r.w0_s)
    take(NL.at[0 : 7 * 32], r.nz_s)
    take(NL.at[0 : 3 * 256], r.nx_s)
    take(W.at[0 : 63 * 48], r.w_s)

    @pl.when(cross)
    def _():
        take(W.at[0:48], r.w_s)

    take(r.p1r.at[0:15], r.p1_s)
    take(r.pmine, r.x_s)
    take(r.gen.at[0:7], r.g_s)
    take(r.gen, r.g_r)
    take(r.R, r.f_r)


def on_device(latents, noise, steps_t, w_in, norm_gain, w_qkv, q_gain, k_gain, w_out):
    gen, grads = pl.pallas_call(
        mega_kernel,
        out_shape=(
            jax.ShapeDtypeStruct((SAMPLES, 8, 128), F32),
            jax.ShapeDtypeStruct((HEADS, 16, TRIPLE), BF),
        ),
        in_specs=[VM, VM, SM, VM, VM, VM, VM, VM, VM],
        out_specs=(VM, VM),
        scratch_shapes=[pltpu.VMEM(*spec) for spec in SCRATCH.values()]
        + [DMA if n is None else DMA(n if isinstance(n, tuple) else (n,)) for n in SEMS.values()],
        compiler_params=pltpu.CompilerParams(
            collective_id=0, has_side_effects=True, vmem_limit_bytes=56 * 1024 * 1024
        ),
        name="distill_step",
    )(latents, noise, steps_t, w_in, norm_gain, w_qkv, q_gain, k_gain, w_out)
    return gen[:, :4, :CH], grads[:, :12, :].astype(F32)


def solution(mesh):
    return jax.shard_map(
        on_device,
        mesh=mesh,
        in_specs=(
            P(None, ("grp", "mp"), None),
            P(None, ("grp", "mp"), None),
            P(),
            P("grp", None, None),
            P("grp", None),
            P("grp", None, "mp", None),
            P("grp", None, None),
            P("grp", None, None),
            P("grp", None, None),
        ),
        out_specs=(P(None, ("grp", "mp"), None), P(None, ("grp", "mp"), None)),
        check_vma=False,
    )
```

```python
import functools
import math

import jax
import jax.numpy as jnp
from jax import lax
from jax.experimental import pallas as pl
from jax.experimental.pallas import tpu as pltpu
from jax.sharding import PartitionSpec as P

MESH = pl.DeviceIdType.MESH
XH, NY, NZ, NC = 2, 4, 8, 2
HEADS, SAMPLES = XH * NZ, NY * NC
D, HD, CH, LEN = 3072, 128, 64, 1024
TRIPLE = 3 * HD
BF, F32 = jnp.bfloat16, jnp.float32


def place():
    m = lax.axis_index("mp")
    return (
        lax.axis_index("grp"),
        m // (NY * NZ * NC),
        (m // (NZ * NC)) % NY,
        (m // NC) % NZ,
        m % NC,
    )


def device(g, xh, y, z, c):
    return (g, ((xh * NY + y) * NZ + z) * NC + c)


def mod(a, n):
    return lax.rem(a, n)


def rows(start, size, step):
    return pl.ds(pl.multiple_of(start, step), size)


def send(src, dst, ssem, rsem, target):
    copy = pltpu.make_async_remote_copy(
        src_ref=src, dst_ref=dst, send_sem=ssem, recv_sem=rsem, device_id=target, device_id_type=MESH
    )
    copy.start()


def take(ref, sem):
    pltpu.make_async_copy(ref, ref, sem).wait()


def greet(barrier, target):
    pl.semaphore_signal(barrier, inc=1, device_id=target, device_id_type=MESH)


Z_ORDER = (0, 1, 7, 2, 6, 3, 5, 4)


DMA = pltpu.SemaphoreType.DMA
VM = pl.BlockSpec(memory_space=pltpu.VMEM)
SM = pl.BlockSpec(memory_space=pltpu.SMEM)
HB = pl.BlockSpec(memory_space=pl.ANY)
HALF, PART = D // 2, 192
TILE = 256
SCALE = 1.0 / math.sqrt(HD)


def dot(a, b, ca=1, cb=0):
    return lax.dot_general(a, b, (((ca,), (cb,)), ((), ())), preferred_element_type=F32)


SCRATCH = dict(
    w_own=((HEADS, 24, TRIPLE), BF),
    w_in=((CH, D), BF),
    w_outT=((CH, HD), BF),
    W=((3, D, HD), BF),
    NL=((LEN, 128), BF),
    w0s=((NZ, 32, TRIPLE), BF),
    w0r=((NZ, 32, TRIPLE), BF),
    w1s=((3, NZ, 48, HD), BF),
    nst=((SAMPLES, 16, 128), BF),
    n1r=((SAMPLES, 16, 128), BF),
    nsf=((SAMPLES, 16, 128), F32),
    n1f=((32, 128), F32),
    temb=((8, D), F32),
    xf=((128, D), F32),
    xn=((LEN, D), BF),
    xnT=((D, LEN), BF),
    qkv=((LEN, TRIPLE), F32),
    qn=((LEN, HD), BF),
    kn=((LEN, HD), BF),
    v=((LEN, HD), BF),
    knT=((HD, LEN), BF),
    vT=((HD, LEN), BF),
    p32=((4, LEN, TILE), F32),
    pb=((4, LEN, TILE), BF),
    pp=((LEN // 2, 128), BF),
    p1r=((HEADS, 32, 128), BF),
    dch=((32, 128), BF),
    cot=((LEN // 2, 128), BF),
    pmine=((32, 128), F32),
    pother=((32, 128), F32),
    gs=((SAMPLES, 8, 128), F32),
    d_att=((LEN, HD), BF),
    dq=((LEN, HD), F32),
    dk=((LEN, HD), F32),
    dqk=((LEN, 2 * HD), BF),
    dv=((LEN, HD), BF),
    gr=((SAMPLES, 8, 128), F32),
    Rf=((HEADS, 16, TRIPLE), F32),
    **{
        name + str(q): (shape[:-1] + (n,), kind)
        for q, n in ((0, HD), (1, 2 * HD))
        for name, shape, kind in (
            ("T", (2, HALF, 0), BF),
            ("sibr", (2, HALF // 2, 0), BF),
            ("yst", (2, NY, XH, PART // 2, 0), BF),
            ("yr", (2, NY, XH, PART // 2, 0), BF),
            ("fin", (PART // 2, 0), F32),
            ("st", (2, XH, 8, 16, 0), BF),
            ("R", (HEADS, 16, 0), BF),
        )
    },
)
SEMS = dict(
    n1_s=None, n1_r=None, nz_s=None, nz_r=None, nx_s=None, nx_r=None, w0_s=None, w0_r=None, w_s=None,
    w1_s=3, w1_r=3, wa_r=3, wb_r=3, wr_r=3, sb_r=3, p1_s=None, p1_r=None, d_s=None, d_r=XH,
    x_s=None, x_r=None, g_s=None, g_r=None, ts_s=2, ts_r=(2, NY, 2), y_s=2,
    y_r=(2, XH, 2), f_s=2, f_r=2, in_r=3,
)
INPUTS = ("lat", "noise", "steps", "w_in_hbm", "gain", "w_qkv", "q_gain", "k_gain", "w_out")


class Refs:
    pass


def mega_kernel(*args):
    r = Refs()
    names = INPUTS + ("gen", "grad") + tuple(SCRATCH) + tuple(SEMS)
    for name, ref in zip(names, args, strict=True):
        setattr(r, name, ref)
    g, xh, y, z, c = place()
    h, me_b, X = xh * NZ + z, y * NC + c, xh * 2 + g
    fake, cross = g == 1, xh != c
    W, NL = r.W, r.NL

    def yc(dy, dc):
        return mod(y + dy, NY), mod(c + dc, NC)

    def zline(dz):
        return device(g, xh, y, mod(z + dz, NZ), c)

    def xline(dx):
        X2 = mod(X + dx, 4)
        return device(mod(X2, 2), X2 // 2, y, z, c)

    loads = (
        pltpu.make_async_copy(r.w_qkv.at[0], r.w_own, r.in_r.at[0]),
        pltpu.make_async_copy(r.w_in_hbm.at[0], r.w_in, r.in_r.at[1]),
        pltpu.make_async_copy(
            r.w_out.at[0, :, pl.ds(pl.multiple_of(h * HD, HD), HD)], r.w_outT, r.in_r.at[2]
        ),
    )
    for load in loads:
        load.start()

    barrier = pltpu.get_barrier_semaphore()
    for dy in range(NY):
        for dc in range(NC):
            if dy or dc:
                y2, c2 = yc(dy, dc)
                greet(barrier, device(g, xh, y2, z, c2))
    for dz in range(1, NZ):
        greet(barrier, zline(dz))
    for dx in range(1, 4):
        greet(barrier, xline(dx))

    @pl.when(cross)
    def _():
        for dz in range(NZ):
            greet(barrier, device(g, c, y, mod(z + dz, NZ), xh))

    loads[0].wait()
    for j in range(NZ):
        r.w0s[j, 0:24, :] = r.w_own[(1 - c) * NZ + j]
        r.w0s[j, 24:32, :] = jnp.zeros((8, TRIPLE), BF)

    rows8 = lax.broadcasted_iota(jnp.int32, (SAMPLES, 128), 0)
    ang = jnp.zeros((SAMPLES, 128), F32)
    for b in range(SAMPLES):
        ang = jnp.where(rows8 == b, r.steps[b].astype(F32), ang)
    ang = 0.5 * math.pi / 1000.0 * ang
    alpha, sigma = jnp.cos(ang), jnp.sin(ang)
    r.nsf[...] = jnp.zeros_like(r.nsf)
    for b in range(SAMPLES):
        latent = r.lat[b].astype(F32)
        noisy = alpha[b : b + 1, 0:CH] * latent + sigma[b : b + 1, 0:CH] * r.noise[b].astype(F32)
        r.nsf[b, 0:4, 0:CH] = noisy
        r.nsf[b, 0:4, CH:128] = latent
    r.nst[...] = r.nsf[...].astype(BF)

    pl.semaphore_wait(barrier, 7 + 7 + 3 + jnp.where(cross, NZ, 0))

    sib = device(g, xh, y, z, 1 - c)
    send(r.w0s, r.w0r, r.w0_s, r.w0_r, sib)
    for dy in range(NY):
        for dc in range(NC):
            y2, c2 = yc(dy, dc)
            src = r.nst.at[y2 * NC + c2]
            if dy or dc:
                send(src, r.n1r.at[me_b], r.n1_s, r.n1_r, device(g, xh, y2, z, c2))
            else:
                pltpu.make_async_copy(src, r.n1r.at[me_b], r.n1_r).start()

    take(r.w0r, r.w0_r)
    for j in range(NZ):
        mine = r.w_own[c * NZ + j].astype(F32)
        theirs = r.w0r[j, 0:24, :].astype(F32)
        low = jnp.where(c == 0, mine, theirs)
        high = jnp.where(c == 0, theirs, mine)
        both = jnp.concatenate([low, high], axis=0).astype(BF)
        for k in range(3):
            r.w1s[k, j] = both[:, k * HD : k * HD + HD]

    def to_heads(k):
        for dz in Z_ORDER:
            z2 = mod(z + dz, NZ)
            src, dst = r.w1s.at[k, z2], W.at[k, rows(((xh * NY + y) * NZ + z) * 48, 48, 48)]
            if dz:
                send(src, dst, r.w1_s.at[k], r.w1_r.at[k], device(g, c, y, z2, xh))
            else:

                @pl.when(cross)
                def _():
                    send(src, dst, r.w1_s.at[k], r.w1_r.at[k], device(g, c, y, z2, xh))

                @pl.when(jnp.logical_not(cross))
                def _():
                    pltpu.make_async_copy(src, dst, r.w1_r.at[k]).start()

    def left(k):
        take(W.at[k, 0 : 7 * 48], r.w1_s.at[k])

        @pl.when(cross)
        def _():
            take(W.at[k, 0:48], r.w1_s.at[k])

    to_heads(0)

    take(r.n1r, r.n1_r)
    for j in range(SAMPLES):
        r.n1f[j * 4 : j * 4 + 4, :] = r.n1r[j, 0:4, :].astype(F32)
    own_n = rows((X * NZ + z) * 32, 32, 32)
    NL[own_n, :] = r.n1f[...].astype(BF)
    for dz in Z_ORDER[1:]:
        send(NL.at[own_n], NL.at[own_n], r.nz_s, r.nz_r, zline(dz))

    up, down = device(g, xh, mod(y + 1, NY), z, c), device(g, xh, mod(y + 3, NY), z, c)

    def chunk(dy, k, off=0, size=2 * PART):
        return W.at[k, rows((c * NY + mod(y + dy, NY)) * 2 * PART + off, size, PART)]

    def pass_on(ref, rsem, target):
        send(ref, ref, r.w_s, rsem, target)

    def relay_own(k):
        ref = chunk(0, k)
        take(ref, r.w1_r.at[k])
        pass_on(ref, r.wa_r.at[k], up)
        pass_on(ref, r.wb_r.at[k], down)
        if k:
            pass_on(ref, r.wr_r.at[k], device(g, xh, mod(y + 2, NY), z, c))
        pass_on(ref, r.sb_r.at[k], sib)

    def relay_near(k):
        take(chunk(3, k), r.wa_r.at[k])
        if k == 0:
            pass_on(chunk(3, k, 0, PART), r.wr_r.at[k], up)
        pass_on(chunk(3, k), r.sb_r.at[k], sib)
        take(chunk(1, k), r.wb_r.at[k])
        if k == 0:
            pass_on(chunk(1, k, PART, PART), r.wr_r.at[k], down)
        pass_on(chunk(1, k), r.sb_r.at[k], sib)

    def relay_far(k):
        take(chunk(2, k), r.wr_r.at[k])
        pass_on(chunk(2, k), r.sb_r.at[k], sib)

    t_value = r.steps[me_b].astype(F32)
    index = lax.broadcasted_iota(jnp.int32, (1, D // 2), 1).astype(F32)
    phase = t_value * jnp.exp(-math.log(10000.0) * index / (D // 2))
    r.temb[0:1, 0 : D // 2] = jnp.sin(phase)
    r.temb[0:1, D // 2 :] = jnp.cos(phase)

    left(0)
    to_heads(1)
    relay_own(0)
    take(NL.at[0 : 7 * 32], r.nz_r)
    own_x = rows(X * 256, 256, 256)
    for dx in range(1, 4):
        send(NL.at[own_x], NL.at[own_x], r.nx_s, r.nx_r, xline(dx))
    left(1)
    to_heads(2)
    loads[1].wait()

    def embed(tile):
        at = rows(tile * 128, 128, 128)
        noisy = NL[at, :][:, 0:CH]
        total = jnp.zeros((128, 128), F32)
        for k in range(D // 512):
            part = dot(noisy, r.w_in[:, k * 512 : k * 512 + 512]) + r.temb[0:1, k * 512 : k * 512 + 512]
            r.xf[:, k * 512 : k * 512 + 512] = part
            sq = part * part
            for i in range(4):
                total = total + sq[:, i * 128 : i * 128 + 128]
        inv = lax.rsqrt(jnp.sum(total, axis=1, keepdims=True) * (1.0 / D) + 1e-06)
        for k in range(D // 512):
            cols = slice(k * 512, k * 512 + 512)
            done = (r.xf[:, cols] * inv * r.gain[0:1, cols]).astype(BF)
            r.xn[at, cols] = done

            @pl.when(fake)
            def _():
                r.xnT[cols, at] = done.T

    steps = {
        0: [(relay_own, 1)], 1: [(relay_near, 0)], 2: [(relay_own, 2), (relay_far, 0)],
        4: [(relay_near, 1)], 5: [(relay_far, 1)], 6: [(relay_near, 2)],
    }
    for i in range(8):
        if i == 2:
            take(NL.at[0 : 3 * 256], r.nx_r)
        embed(mod(X * 2 + i, 8))
        for step, k in steps.get(i, ()):
            step(k)

    def project(half, first, lanes, ks):
        cols = rows(half * HALF, HALF, HALF)
        weight = jnp.concatenate([W[k, cols, :] for k in ks], axis=1)
        for i in range(4):
            at = slice(i * TILE, i * TILE + TILE)
            part = dot(r.xn[at, cols], weight)
            r.qkv[at, lanes] = part if first else r.qkv[at, lanes] + part

    qk_l, v_l = slice(0, 2 * HD), slice(2 * HD, TRIPLE)
    project(c, True, qk_l, (0, 1))
    for k in range(2):
        take(W.at[k, 0:HALF], r.sb_r.at[k])
    project(1 - c, False, qk_l, (0, 1))
    relay_far(2)

    gain_q, gain_k = r.q_gain[0, pl.ds(h, 1), :], r.k_gain[0, pl.ds(h, 1), :]

    def normed(lanes):
        raw = r.qkv[:, lanes]
        inv = lax.rsqrt(jnp.mean(raw * raw, axis=-1, keepdims=True) + 1e-06)
        return raw, inv

    q_l, k_l = slice(0, HD), slice(HD, 2 * HD)
    raw, inv = normed(q_l)
    r.qn[...] = (raw * inv * gain_q).astype(BF)
    raw, inv = normed(k_l)
    k_norm = (raw * inv * gain_k).astype(BF)
    r.kn[...] = k_norm
    r.knT[...] = k_norm.T
    for t in range(4):
        at = slice(t * TILE, t * TILE + TILE)
        scores = dot(r.kn[...], r.qn[at, :], 1, 1)
        expo = jnp.exp2(scores * (SCALE * math.log2(math.e)))
        probs = expo * (1.0 / jnp.sum(expo, axis=0, keepdims=True))
        r.p32[t] = probs
        r.pb[t] = probs.astype(BF)

    project(c, True, v_l, (2,))
    take(W.at[2, 0:HALF], r.sb_r.at[2])
    project(1 - c, False, v_l, (2,))
    value = r.qkv[:, v_l].astype(BF)
    r.v[...] = value
    r.vT[...] = value.T
    loads[2].wait()

    halves = []
    for t in range(4):
        attended = dot(r.vT[...], r.pb[t]).astype(BF)
        halves.append(dot(r.w_outT[...], attended).T)
        if t % 2 == 1:
            x2 = t // 2
            r.pp[x2 * 256 : x2 * 256 + 256, :] = jnp.concatenate(halves, axis=1).astype(BF)
            halves = []
            for dz in Z_ORDER:
                z2 = mod(z + dz, NZ)
                src, dst = r.pp.at[rows((x2 * NZ + z2) * 32, 32, 32)], r.p1r.at[h]
                if dz:
                    send(src, dst, r.p1_s, r.p1_r, device(g, x2, y, z2, c))
                else:

                    @pl.when(xh == x2)
                    def _():
                        pltpu.make_async_copy(src, dst, r.p1_r).start()

                    @pl.when(xh != x2)
                    def _():
                        send(src, dst, r.p1_s, r.p1_r, device(g, x2, y, z2, c))

    take(r.p1r, r.p1_r)
    pred = jnp.sum(r.p1r[...].astype(F32), axis=0)
    r.pmine[...] = pred

    @pl.when(fake)
    def _():
        lat0 = NL[rows((xh * 2 * NZ + z) * 32, 32, 32), :].astype(F32)[:, CH:]
        lat1 = NL[rows(((xh * 2 + 1) * NZ + z) * 32, 32, 32), :].astype(F32)[:, CH:]
        latent = jnp.concatenate([lat0, lat1], axis=1)
        r.dch[...] = ((pred - latent) * (1.0 / SAMPLES)).astype(BF)
        own = rows(h * 32, 32, 32)
        for dx in range(XH):
            for dz in Z_ORDER:
                if dx or dz:
                    target = device(g, mod(xh + dx, XH), y, mod(z + dz, NZ), c)
                    send(r.dch, r.cot.at[own], r.d_s, r.d_r.at[xh], target)
        pltpu.make_async_copy(r.dch, r.cot.at[own], r.d_r.at[xh]).start()

    partner = device(1 - g, xh, y, z, c)
    send(r.pmine, r.pother, r.x_s, r.x_r, partner)

    def generator():
        take(r.pother, r.x_r)
        diff = jnp.where(g == 0, r.pother[...] - r.pmine[...], r.pmine[...] - r.pother[...])
        mine = jnp.where(g == 0, diff[:, 0:CH], diff[:, CH:])
        for j in range(SAMPLES):
            r.gs[j, 0:4, 0:CH] = mine[j * 4 : j * 4 + 4, :]
        for dy in range(NY):
            for dc in range(NC):
                y2, c2 = yc(dy, dc)
                src, dst = r.gs.at[y2 * NC + c2], r.gr.at[me_b]
                if dy or dc:
                    send(src, dst, r.g_s, r.g_r, device(g, xh, y2, z, c2))
                else:
                    pltpu.make_async_copy(src, dst, r.g_r).start()

    def deliver(q, zh, slot, net, x2, head):
        yr, fin, st, R = (getattr(r, name + str(q)) for name in ("yr", "fin", "st", "R"))
        take(yr.at[zh, :, slot], r.y_r.at[q, slot, zh])
        fin[...] = jnp.sum(yr[zh, :, slot].astype(F32), axis=0)
        for i in range(8):
            st[zh, slot, i, 0:12, :] = fin[i * 12 : i * 12 + 12, :].astype(BF)
        fs, fr = r.f_s.at[q], r.f_r.at[q]
        for e in range(4):
            zq, zr = mod(z // 4 + e // 2, 2), mod(z + e, 2)
            z2 = zq * 4 + zh * 2 + zr
            for c2 in range(NC):
                src, dst = st.at[zh, slot, (zq * 2 + zr) * NC + c2], R.at[head]
                target = device(net, x2, y, z2, c2)
                if e:
                    send(src, dst, fs, fr, target)
                else:
                    me = (x2 == xh) & (c2 == c) & (z2 == z)

                    @pl.when(me)
                    def _():
                        pltpu.make_async_copy(src, dst, fr).start()

                    @pl.when(jnp.logical_not(me))
                    def _():
                        send(src, dst, fs, fr, target)


    @pl.when(jnp.logical_not(fake))
    def _():
        generator()
        for q in range(2):
            for zh in range(2):
                deliver(q, zh, 0, 0, xh, c * NZ + z)
        for q in range(2):
            take(getattr(r, f"R{q}").at[0:15], r.f_s.at[q])

    @pl.when(fake)
    def _():
        for t in range(4):
            if t % 2 == 0:
                take(r.cot.at[0:256], r.d_r.at[t // 2])
            at = slice(t * TILE, t * TILE + TILE)
            cot = r.cot[(t // 2) * 256 : (t // 2) * 256 + 256, (t % 2) * CH : (t % 2) * CH + CH]
            r.d_att[at, :] = dot(cot, r.w_outT[...]).astype(BF)
        dv = dot(r.pb[0], r.d_att[0:TILE, :])
        for t in range(1, 4):
            dv = dv + dot(r.pb[t], r.d_att[t * TILE : t * TILE + TILE, :])
        r.dv[...] = dv.astype(BF)

        def scores_back(t):
            at = slice(t * TILE, t * TILE + TILE)
            d_probs = dot(r.v[...], r.d_att[at, :], 1, 1)
            probs = r.p32[t]
            mean = jnp.sum(probs * d_probs, axis=0, keepdims=True)
            d_score = (probs * (d_probs - mean)).astype(BF)
            dk = dot(d_score, r.qn[at, :])
            if t:
                r.dk[...] += dk
            else:
                r.dk[...] = dk
            r.dq[at, :] = dot(r.knT[...], d_score).T

        def unnorm(lanes, gain, grad):
            raw, inv = normed(lanes)
            scaled = grad * SCALE * gain
            unit = raw * inv
            inner = jnp.mean(unit * scaled, axis=-1, keepdims=True)
            r.dqk[:, lanes] = (inv * (scaled - unit * inner)).astype(BF)

        def place_of(j, x2):
            return (x2 * NY + mod(y + j, NY)) * (PART // 2)

        class Lanes:
            def __init__(self, q, grad):
                self.q, self.grad = q, grad
                for name in ("T", "sibr", "yst", "yr", "R"):
                    setattr(self, name, getattr(r, name + str(q)))

            def block(self, half, zh, js):
                pairs = [(j, x2) for j in js for x2 in range(XH)]
                left = []
                for j, x2 in pairs:
                    first = half * HALF + (x2 * NY + mod(y + j, NY)) * PART + zh * 48
                    left += [r.xnT[rows(first + zq * 96, 48, 48), :] for zq in range(2)]
                out = dot(jnp.concatenate(left, axis=0), self.grad[...]).astype(BF)
                for i, (j, x2) in enumerate(pairs):
                    at = rows(half * (HALF // 2) + place_of(j, x2), 96, 96)
                    self.T[zh, at, :] = out[i * 96 : i * 96 + 96]

            def to_sibling(self, zh, js):
                self.block(1 - c, zh, js)
                for j in js:
                    for x2 in range(XH):
                        src = self.T.at[zh, rows((1 - c) * (HALF // 2) + place_of(j, x2), 96, 96)]
                        dst = self.sibr.at[zh, rows(place_of(j, x2), 96, 96)]
                        send(src, dst, r.ts_s.at[self.q], r.ts_r.at[self.q, j, zh], sib)

            def chunks_out(self, zh, js):
                ys = r.y_s.at[self.q]
                for j in js:
                    take(self.sibr.at[zh, 0:PART], r.ts_r.at[self.q, j, zh])
                    for x2 in range(XH):
                        mine = self.T[zh, rows(c * (HALF // 2) + place_of(j, x2), 96, 96), :]
                        theirs = self.sibr[zh, rows(place_of(j, x2), 96, 96), :]
                        src = self.yst.at[zh, j, x2]
                        src[...] = (mine.astype(F32) + theirs.astype(F32)).astype(BF)

                        @pl.when(c == 0)
                        def _():
                            target = device(0, x2, mod(y + j, NY), z, xh)
                            send(src, self.yr.at[zh, j, 0], ys, r.y_r.at[self.q, 0, zh], target)

                        @pl.when(c == 1)
                        def _():
                            dst, arrive = self.yr.at[zh, j, x2], r.y_r.at[self.q, x2, zh]
                            if j:
                                send(src, dst, ys, arrive, device(1, xh, mod(y + j, NY), z, 1))
                            else:
                                pltpu.make_async_copy(src, dst, arrive).start()

            def drain(self):
                take(self.sibr, r.ts_s.at[self.q])
                take(self.yst.at[:, 0:3], r.y_s.at[self.q])

                @pl.when(c == 0)
                def _():
                    take(self.yst.at[:, 3], r.y_s.at[self.q])

        a, b = Lanes(0, r.dv), Lanes(1, r.dqk)
        near, rest = (2, 1), (3, 0)
        a.to_sibling(0, near)
        a.to_sibling(0, rest)
        a.block(c, 0, near)
        a.block(c, 0, rest)
        a.chunks_out(0, near)
        a.to_sibling(1, near)
        a.to_sibling(1, rest)
        a.chunks_out(0, rest)
        a.block(c, 1, near)
        a.block(c, 1, rest)
        a.chunks_out(1, near + rest)
        for t in range(4):
            scores_back(t)
        unnorm(q_l, gain_q, r.dq[...])
        unnorm(k_l, gain_k, r.dk[...])
        b.to_sibling(0, near)
        b.to_sibling(0, rest)
        b.block(c, 0, near)
        b.block(c, 0, rest)
        b.chunks_out(0, near)
        b.to_sibling(1, near)
        b.chunks_out(0, rest)
        b.to_sibling(1, rest)
        b.block(c, 1, near)
        b.block(c, 1, rest)
        b.chunks_out(1, near + rest)
        generator()

        @pl.when(c == 1)
        def _():
            for q in range(2):
                for zh in range(2):
                    for x2 in range(XH):
                        deliver(q, zh, x2, 1, x2, h)
            for R, fs in ((r.R0, r.f_s.at[0]), (r.R1, r.f_s.at[1])):
                take(R, fs)
                take(R.at[0:15], fs)

        a.drain()
        b.drain()
        take(r.cot.at[0 : 15 * 32], r.d_s)

    take(r.n1r.at[0:7], r.n1_s)
    take(r.w0s, r.w0_s)
    take(NL.at[0 : 7 * 32], r.nz_s)
    take(NL.at[0 : 3 * 256], r.nx_s)
    for k in range(3):
        if k == 2:
            left(2)
        take(W.at[k, 0 : 7 * 2 * PART], r.w_s)

    take(r.p1r.at[0:15], r.p1_s)
    take(r.pmine, r.x_s)
    take(r.gr.at[0:7], r.g_s)
    take(r.gr, r.g_r)
    r.gen[...] = r.gr[:, 0:4, 0:CH]
    take(r.R0, r.f_r.at[0])
    r.Rf[:, :, v_l] = r.R0[...].astype(F32)
    take(r.R1, r.f_r.at[1])
    r.Rf[:, :, qk_l] = r.R1[...].astype(F32)
    for i in range(12):
        r.grad[i] = r.Rf[:, i, :]


def on_device(latents, noise, steps_t, w_in, norm_gain, w_qkv, q_gain, k_gain, w_out):
    gen, grads = pl.pallas_call(
        mega_kernel,
        out_shape=(
            jax.ShapeDtypeStruct((SAMPLES, 4, CH), F32),
            jax.ShapeDtypeStruct((12, HEADS, TRIPLE), F32),
        ),
        in_specs=[VM, VM, SM, HB, VM, HB, VM, VM, HB],
        out_specs=(VM, VM),
        scratch_shapes=[pltpu.VMEM(*spec) for spec in SCRATCH.values()]
        + [DMA if n is None else DMA(n if isinstance(n, tuple) else (n,)) for n in SEMS.values()],
        compiler_params=pltpu.CompilerParams(
            collective_id=0, has_side_effects=True, vmem_limit_bytes=58 * 1024 * 1024
        ),
        name="distill_step",
    )(latents, noise, steps_t, w_in, norm_gain, w_qkv, q_gain, k_gain, w_out.transpose(0, 2, 1))
    return gen, grads.transpose(1, 0, 2)


def solution(mesh):
    return jax.shard_map(
        on_device,
        mesh=mesh,
        in_specs=(
            P(None, ("grp", "mp"), None),
            P(None, ("grp", "mp"), None),
            P(),
            P("grp", None, None),
            P("grp", None),
            P("grp", None, "mp", None),
            P("grp", None, None),
            P("grp", None, None),
            P("grp", None, None),
        ),
        out_specs=(P(None, ("grp", "mp"), None), P(None, ("grp", "mp"), None)),
        check_vma=False,
    )
```

```python
import functools
import math

import jax
import jax.numpy as jnp
from jax import lax
from jax.experimental import pallas as pl
from jax.experimental.pallas import tpu as pltpu
from jax.sharding import PartitionSpec as P

MESH = pl.DeviceIdType.MESH
XH, NY, NZ, NC = 2, 4, 8, 2
HEADS, SAMPLES = XH * NZ, NY * NC
D, HD, CH, LEN = 3072, 128, 64, 1024
TRIPLE = 3 * HD
BF, F32 = jnp.bfloat16, jnp.float32


def place():
    m = lax.axis_index("mp")
    return (
        lax.axis_index("grp"),
        m // (NY * NZ * NC),
        (m // (NZ * NC)) % NY,
        (m // NC) % NZ,
        m % NC,
    )


def device(g, xh, y, z, c):
    return (g, ((xh * NY + y) * NZ + z) * NC + c)


def mod(a, n):
    return lax.rem(a, n)


def rows(start, size, step):
    return pl.ds(pl.multiple_of(start, step), size)


def send(src, dst, ssem, rsem, target):
    copy = pltpu.make_async_remote_copy(
        src_ref=src, dst_ref=dst, send_sem=ssem, recv_sem=rsem, device_id=target, device_id_type=MESH
    )
    copy.start()


def take(ref, sem):
    pltpu.make_async_copy(ref, ref, sem).wait()


def greet(barrier, target):
    pl.semaphore_signal(barrier, inc=1, device_id=target, device_id_type=MESH)


Z_ORDER = (0, 1, 7, 2, 6, 3, 5, 4)


DMA = pltpu.SemaphoreType.DMA
VM = pl.BlockSpec(memory_space=pltpu.VMEM)
SM = pl.BlockSpec(memory_space=pltpu.SMEM)
HB = pl.BlockSpec(memory_space=pl.ANY)
HALF, PART = D // 2, 192
TILE = 256
SCALE = 1.0 / math.sqrt(HD)


def dot(a, b, ca=1, cb=0):
    return lax.dot_general(a, b, (((ca,), (cb,)), ((), ())), preferred_element_type=F32)


SCRATCH = dict(
    lat=((SAMPLES, 4, CH), BF),
    noise=((SAMPLES, 4, CH), BF),
    gain=((1, D), F32),
    q_gain=((1, HEADS, HD), F32),
    k_gain=((1, HEADS, HD), F32),
    w_own=((HEADS, 24, TRIPLE), BF),
    w_in=((CH, D), BF),
    w_outT=((CH, HD), BF),
    W=((3, D, HD), BF),
    NL=((LEN, 128), BF),
    w0s=((NZ, 32, TRIPLE), BF),
    w0r=((NZ, 32, TRIPLE), BF),
    w1s=((3, NZ, 48, HD), BF),
    nst=((SAMPLES, 16, 128), BF),
    n1r=((SAMPLES, 16, 128), BF),
    nsf=((SAMPLES, 16, 128), F32),
    n1f=((32, 128), F32),
    temb=((8, D), F32),
    xf=((128, D), F32),
    xn=((LEN, D), BF),
    xnT=((D, LEN), BF),
    qkv=((LEN, TRIPLE), F32),
    qn=((LEN, HD), BF),
    kn=((LEN, HD), BF),
    v=((LEN, HD), BF),
    knT=((HD, LEN), BF),
    vT=((HD, LEN), BF),
    p32=((4, LEN, TILE), F32),
    pb=((4, LEN, TILE), BF),
    pp=((LEN // 2, 128), BF),
    p1r=((HEADS, 32, 128), BF),
    dch=((32, 128), BF),
    cot=((LEN // 2, 128), BF),
    pmine=((32, 128), F32),
    pother=((32, 128), F32),
    gs=((SAMPLES, 8, 128), F32),
    d_att=((LEN, HD), BF),
    dq=((LEN, HD), F32),
    dk=((LEN, HD), F32),
    dqk=((LEN, 2 * HD), BF),
    dv=((LEN, HD), BF),
    gr=((SAMPLES, 8, 128), F32),
    Rf=((HEADS, 16, TRIPLE), F32),
    **{
        name + str(q): (shape[:-1] + (n,), kind)
        for q, n in ((0, HD), (1, 2 * HD))
        for name, shape, kind in (
            ("T", (2, HALF, 0), BF),
            ("sibr", (2, HALF // 2, 0), BF),
            ("yst", (2, NY, XH, PART // 2, 0), BF),
            ("yr", (2, NY, XH, PART // 2, 0), BF),
            ("fin", (PART // 2, 0), F32),
            ("st", (2, XH, 8, 16, 0), BF),
            ("R", (HEADS, 16, 0), BF),
        )
    },
)
SEMS = dict(
    n1_s=None, n1_r=None, nz_s=None, nz_r=None, nx_s=None, nx_r=None, w0_s=None, w0_r=None, w_s=None,
    w1_s=3, w1_r=3, wa_r=3, wb_r=3, wr_r=3, sb_r=3, p1_s=None, p1_r=None, d_s=None, d_r=XH,
    x_s=None, x_r=None, g_s=None, g_r=None, ts_s=2, ts_r=(2, NY, 2), y_s=2,
    y_r=(2, XH, 2), f_s=2, f_r=2, in_r=8,
)
INPUTS = (
    "lat_hbm", "noise_hbm", "steps", "w_in_hbm", "gain_hbm", "w_qkv", "q_gain_hbm", "k_gain_hbm", "w_out"
)


class Refs:
    pass


def mega_kernel(*args):
    r = Refs()
    names = INPUTS + ("gen", "grad") + tuple(SCRATCH) + tuple(SEMS)
    for name, ref in zip(names, args, strict=True):
        setattr(r, name, ref)
    g, xh, y, z, c = place()
    h, me_b, X = xh * NZ + z, y * NC + c, xh * 2 + g
    fake, cross = g == 1, xh != c
    W, NL = r.W, r.NL

    def yc(dy, dc):
        return mod(y + dy, NY), mod(c + dc, NC)

    def zline(dz):
        return device(g, xh, y, mod(z + dz, NZ), c)

    def xline(dx):
        X2 = mod(X + dx, 4)
        return device(mod(X2, 2), X2 // 2, y, z, c)

    barrier = pltpu.get_barrier_semaphore()
    for dy in range(NY):
        for dc in range(NC):
            if dy or dc:
                y2, c2 = yc(dy, dc)
                greet(barrier, device(g, xh, y2, z, c2))
    for dz in range(1, NZ):
        greet(barrier, zline(dz))
    for dx in range(1, 4):
        greet(barrier, xline(dx))

    @pl.when(cross)
    def _():
        for dz in range(NZ):
            greet(barrier, device(g, c, y, mod(z + dz, NZ), xh))

    loads = (
        pltpu.make_async_copy(r.w_qkv.at[0], r.w_own, r.in_r.at[0]),
        pltpu.make_async_copy(r.w_in_hbm.at[0], r.w_in, r.in_r.at[1]),
        pltpu.make_async_copy(
            r.w_out.at[0, :, pl.ds(pl.multiple_of(h * HD, HD), HD)], r.w_outT, r.in_r.at[2]
        ),
        pltpu.make_async_copy(r.lat_hbm, r.lat, r.in_r.at[3]),
        pltpu.make_async_copy(r.noise_hbm, r.noise, r.in_r.at[4]),
        pltpu.make_async_copy(r.gain_hbm, r.gain, r.in_r.at[5]),
        pltpu.make_async_copy(r.q_gain_hbm, r.q_gain, r.in_r.at[6]),
        pltpu.make_async_copy(r.k_gain_hbm, r.k_gain, r.in_r.at[7]),
    )
    for load in loads:
        load.start()

    loads[0].wait()
    for j in range(NZ):
        r.w0s[j, 0:24, :] = r.w_own[(1 - c) * NZ + j]
        r.w0s[j, 24:32, :] = jnp.zeros((8, TRIPLE), BF)

    loads[3].wait()
    loads[4].wait()
    rows8 = lax.broadcasted_iota(jnp.int32, (SAMPLES, 128), 0)
    ang = jnp.zeros((SAMPLES, 128), F32)
    for b in range(SAMPLES):
        ang = jnp.where(rows8 == b, r.steps[b].astype(F32), ang)
    ang = 0.5 * math.pi / 1000.0 * ang
    alpha, sigma = jnp.cos(ang), jnp.sin(ang)
    r.nsf[...] = jnp.zeros_like(r.nsf)
    r.gs[...] = jnp.zeros_like(r.gs)
    for b in range(SAMPLES):
        latent = r.lat[b].astype(F32)
        noisy = alpha[b : b + 1, 0:CH] * latent + sigma[b : b + 1, 0:CH] * r.noise[b].astype(F32)
        r.nsf[b, 0:4, 0:CH] = noisy
        r.nsf[b, 0:4, CH:128] = latent
    r.nst[...] = r.nsf[...].astype(BF)

    pl.semaphore_wait(barrier, 7 + 7 + 3 + jnp.where(cross, NZ, 0))

    sib = device(g, xh, y, z, 1 - c)
    send(r.w0s, r.w0r, r.w0_s, r.w0_r, sib)
    for dy in range(NY):
        for dc in range(NC):
            y2, c2 = yc(dy, dc)
            src = r.nst.at[y2 * NC + c2]
            if dy or dc:
                send(src, r.n1r.at[me_b], r.n1_s, r.n1_r, device(g, xh, y2, z, c2))
            else:
                pltpu.make_async_copy(src, r.n1r.at[me_b], r.n1_r).start()

    take(r.w0r, r.w0_r)
    for j in range(NZ):
        mine = r.w_own[c * NZ + j].astype(F32)
        theirs = r.w0r[j, 0:24, :].astype(F32)
        low = jnp.where(c == 0, mine, theirs)
        high = jnp.where(c == 0, theirs, mine)
        both = jnp.concatenate([low, high], axis=0).astype(BF)
        for k in range(3):
            r.w1s[k, j] = both[:, k * HD : k * HD + HD]

    def to_heads(k):
        for dz in Z_ORDER:
            z2 = mod(z + dz, NZ)
            src, dst = r.w1s.at[k, z2], W.at[k, rows(((xh * NY + y) * NZ + z) * 48, 48, 48)]
            if dz:
                send(src, dst, r.w1_s.at[k], r.w1_r.at[k], device(g, c, y, z2, xh))
            else:

                @pl.when(cross)
                def _():
                    send(src, dst, r.w1_s.at[k], r.w1_r.at[k], device(g, c, y, z2, xh))

                @pl.when(jnp.logical_not(cross))
                def _():
                    pltpu.make_async_copy(src, dst, r.w1_r.at[k]).start()

    def left(k):
        take(W.at[k, 0 : 7 * 48], r.w1_s.at[k])

        @pl.when(cross)
        def _():
            take(W.at[k, 0:48], r.w1_s.at[k])

    to_heads(0)

    take(r.n1r, r.n1_r)
    for j in range(SAMPLES):
        r.n1f[j * 4 : j * 4 + 4, :] = r.n1r[j, 0:4, :].astype(F32)
    own_n = rows((X * NZ + z) * 32, 32, 32)
    NL[own_n, :] = r.n1f[...].astype(BF)
    for dz in Z_ORDER[1:]:
        send(NL.at[own_n], NL.at[own_n], r.nz_s, r.nz_r, zline(dz))

    up, down = device(g, xh, mod(y + 1, NY), z, c), device(g, xh, mod(y + 3, NY), z, c)

    def chunk(dy, k, off=0, size=2 * PART):
        return W.at[k, rows((c * NY + mod(y + dy, NY)) * 2 * PART + off, size, PART)]

    def pass_on(ref, rsem, target):
        send(ref, ref, r.w_s, rsem, target)

    def relay_own(k):
        ref = chunk(0, k)
        take(ref, r.w1_r.at[k])
        pass_on(ref, r.wa_r.at[k], up)
        pass_on(ref, r.wb_r.at[k], down)
        if k:
            pass_on(ref, r.wr_r.at[k], device(g, xh, mod(y + 2, NY), z, c))
        pass_on(ref, r.sb_r.at[k], sib)

    def relay_near(k):
        take(chunk(3, k), r.wa_r.at[k])
        if k == 0:
            pass_on(chunk(3, k, 0, PART), r.wr_r.at[k], up)
        pass_on(chunk(3, k), r.sb_r.at[k], sib)
        take(chunk(1, k), r.wb_r.at[k])
        if k == 0:
            pass_on(chunk(1, k, PART, PART), r.wr_r.at[k], down)
        pass_on(chunk(1, k), r.sb_r.at[k], sib)

    def relay_far(k):
        take(chunk(2, k), r.wr_r.at[k])
        pass_on(chunk(2, k), r.sb_r.at[k], sib)

    t_value = r.steps[me_b].astype(F32)
    index = lax.broadcasted_iota(jnp.int32, (1, D // 2), 1).astype(F32)
    phase = t_value * jnp.exp(-math.log(10000.0) * index / (D // 2))
    r.temb[0:1, 0 : D // 2] = jnp.sin(phase)
    r.temb[0:1, D // 2 :] = jnp.cos(phase)

    left(0)
    to_heads(1)
    relay_own(0)
    take(NL.at[0 : 7 * 32], r.nz_r)
    own_x = rows(X * 256, 256, 256)
    for dx in range(1, 4):
        send(NL.at[own_x], NL.at[own_x], r.nx_s, r.nx_r, xline(dx))
    left(1)
    to_heads(2)
    for i in (1, 5, 6, 7):
        loads[i].wait()

    def embed(tile):
        at = rows(tile * 128, 128, 128)
        noisy = NL[at, :][:, 0:CH]
        total = jnp.zeros((128, 128), F32)
        for k in range(D // 512):
            part = dot(noisy, r.w_in[:, k * 512 : k * 512 + 512]) + r.temb[0:1, k * 512 : k * 512 + 512]
            r.xf[:, k * 512 : k * 512 + 512] = part
            sq = part * part
            for i in range(4):
                total = total + sq[:, i * 128 : i * 128 + 128]
        inv = lax.rsqrt(jnp.sum(total, axis=1, keepdims=True) * (1.0 / D) + 1e-06)
        for k in range(D // 512):
            cols = slice(k * 512, k * 512 + 512)
            done = (r.xf[:, cols] * inv * r.gain[0:1, cols]).astype(BF)
            r.xn[at, cols] = done

            @pl.when(fake)
            def _():
                r.xnT[cols, at] = done.T

    steps = {
        0: [(relay_own, 1)], 1: [(relay_near, 0)], 2: [(relay_own, 2), (relay_far, 0)],
        4: [(relay_near, 1)], 5: [(relay_far, 1)], 6: [(relay_near, 2)],
    }
    for i in range(8):
        if i == 2:
            take(NL.at[0 : 3 * 256], r.nx_r)
        embed(mod(X * 2 + i, 8))
        for step, k in steps.get(i, ()):
            step(k)

    def project(half, first, lanes, ks):
        cols = rows(half * HALF, HALF, HALF)
        weight = jnp.concatenate([W[k, cols, :] for k in ks], axis=1)
        for i in range(4):
            at = slice(i * TILE, i * TILE + TILE)
            part = dot(r.xn[at, cols], weight)
            r.qkv[at, lanes] = part if first else r.qkv[at, lanes] + part

    qk_l, v_l = slice(0, 2 * HD), slice(2 * HD, TRIPLE)
    project(c, True, qk_l, (0, 1))
    for k in range(2):
        take(W.at[k, 0:HALF], r.sb_r.at[k])
    project(1 - c, False, qk_l, (0, 1))
    relay_far(2)

    gain_q, gain_k = r.q_gain[0, pl.ds(h, 1), :], r.k_gain[0, pl.ds(h, 1), :]

    def normed(lanes):
        raw = r.qkv[:, lanes]
        inv = lax.rsqrt(jnp.mean(raw * raw, axis=-1, keepdims=True) + 1e-06)
        return raw, inv

    q_l, k_l = slice(0, HD), slice(HD, 2 * HD)
    raw, inv = normed(q_l)
    r.qn[...] = (raw * inv * gain_q).astype(BF)
    raw, inv = normed(k_l)
    k_norm = (raw * inv * gain_k).astype(BF)
    r.kn[...] = k_norm
    r.knT[...] = k_norm.T
    for t in range(4):
        at = slice(t * TILE, t * TILE + TILE)
        scores = dot(r.kn[...], r.qn[at, :], 1, 1)
        expo = jnp.exp2(scores * (SCALE * math.log2(math.e)))
        probs = expo * (1.0 / jnp.sum(expo, axis=0, keepdims=True))
        r.p32[t] = probs
        r.pb[t] = probs.astype(BF)

    project(c, True, v_l, (2,))
    take(W.at[2, 0:HALF], r.sb_r.at[2])
    project(1 - c, False, v_l, (2,))
    value = r.qkv[:, v_l].astype(BF)
    r.v[...] = value
    r.vT[...] = value.T
    loads[2].wait()

    halves = []
    for t in range(4):
        attended = dot(r.vT[...], r.pb[t]).astype(BF)
        halves.append(dot(r.w_outT[...], attended).T)
        if t % 2 == 1:
            x2 = t // 2
            r.pp[x2 * 256 : x2 * 256 + 256, :] = jnp.concatenate(halves, axis=1).astype(BF)
            halves = []
            for dz in Z_ORDER:
                z2 = mod(z + dz, NZ)
                src, dst = r.pp.at[rows((x2 * NZ + z2) * 32, 32, 32)], r.p1r.at[h]
                if dz:
                    send(src, dst, r.p1_s, r.p1_r, device(g, x2, y, z2, c))
                else:

                    @pl.when(xh == x2)
                    def _():
                        pltpu.make_async_copy(src, dst, r.p1_r).start()

                    @pl.when(xh != x2)
                    def _():
                        send(src, dst, r.p1_s, r.p1_r, device(g, x2, y, z2, c))

    take(r.p1r, r.p1_r)
    pred = jnp.sum(r.p1r[...].astype(F32), axis=0)
    r.pmine[...] = pred

    @pl.when(fake)
    def _():
        lat0 = NL[rows((xh * 2 * NZ + z) * 32, 32, 32), :].astype(F32)[:, CH:]
        lat1 = NL[rows(((xh * 2 + 1) * NZ + z) * 32, 32, 32), :].astype(F32)[:, CH:]
        latent = jnp.concatenate([lat0, lat1], axis=1)
        r.dch[...] = ((pred - latent) * (1.0 / SAMPLES)).astype(BF)
        own = rows(h * 32, 32, 32)
        for dx in range(XH):
            for dz in Z_ORDER:
                if dx or dz:
                    target = device(g, mod(xh + dx, XH), y, mod(z + dz, NZ), c)
                    send(r.dch, r.cot.at[own], r.d_s, r.d_r.at[xh], target)
        pltpu.make_async_copy(r.dch, r.cot.at[own], r.d_r.at[xh]).start()

    partner = device(1 - g, xh, y, z, c)
    send(r.pmine, r.pother, r.x_s, r.x_r, partner)

    def generator():
        take(r.pother, r.x_r)
        diff = jnp.where(g == 0, r.pother[...] - r.pmine[...], r.pmine[...] - r.pother[...])
        mine = jnp.where(g == 0, diff[:, 0:CH], diff[:, CH:])
        for j in range(SAMPLES):
            r.gs[j, 0:4, 0:CH] = mine[j * 4 : j * 4 + 4, :]
        for dy in range(NY):
            for dc in range(NC):
                y2, c2 = yc(dy, dc)
                src, dst = r.gs.at[y2 * NC + c2], r.gr.at[me_b]
                if dy or dc:
                    send(src, dst, r.g_s, r.g_r, device(g, xh, y2, z, c2))
                else:
                    pltpu.make_async_copy(src, dst, r.g_r).start()

    def deliver(q, zh, slot, net, x2, head):
        yr, fin, st, R = (getattr(r, name + str(q)) for name in ("yr", "fin", "st", "R"))
        take(yr.at[zh, :, slot], r.y_r.at[q, slot, zh])
        fin[...] = jnp.sum(yr[zh, :, slot].astype(F32), axis=0)
        for i in range(8):
            st[zh, slot, i, 0:12, :] = fin[i * 12 : i * 12 + 12, :].astype(BF)
        fs, fr = r.f_s.at[q], r.f_r.at[q]
        for e in range(4):
            zq, zr = mod(z // 4 + e // 2, 2), mod(z + e, 2)
            z2 = zq * 4 + zh * 2 + zr
            for c2 in range(NC):
                src, dst = st.at[zh, slot, (zq * 2 + zr) * NC + c2], R.at[head]
                target = device(net, x2, y, z2, c2)
                if e:
                    send(src, dst, fs, fr, target)
                else:
                    me = (x2 == xh) & (c2 == c) & (z2 == z)

                    @pl.when(me)
                    def _():
                        pltpu.make_async_copy(src, dst, fr).start()

                    @pl.when(jnp.logical_not(me))
                    def _():
                        send(src, dst, fs, fr, target)


    @pl.when(jnp.logical_not(fake))
    def _():
        generator()
        for q in (1, 0):
            for zh in range(2):
                deliver(q, zh, 0, 0, xh, c * NZ + z)
        for q in range(2):
            take(getattr(r, f"R{q}").at[0:15], r.f_s.at[q])

    @pl.when(fake)
    def _():
        for t in range(4):
            if t % 2 == 0:
                take(r.cot.at[0:256], r.d_r.at[t // 2])
            at = slice(t * TILE, t * TILE + TILE)
            cot = r.cot[(t // 2) * 256 : (t // 2) * 256 + 256, (t % 2) * CH : (t % 2) * CH + CH]
            r.d_att[at, :] = dot(cot, r.w_outT[...]).astype(BF)
        def scores_back(t):
            at = slice(t * TILE, t * TILE + TILE)
            d_probs = dot(r.v[...], r.d_att[at, :], 1, 1)
            probs = r.p32[t]
            mean = jnp.sum(probs * d_probs, axis=0, keepdims=True)
            d_score = (probs * (d_probs - mean)).astype(BF)
            dk = dot(d_score, r.qn[at, :])
            if t:
                r.dk[...] += dk
            else:
                r.dk[...] = dk
            r.dq[at, :] = dot(r.knT[...], d_score).T

        def unnorm(lanes, gain, grad):
            raw, inv = normed(lanes)
            scaled = grad * SCALE * gain
            unit = raw * inv
            inner = jnp.mean(unit * scaled, axis=-1, keepdims=True)
            r.dqk[:, lanes] = (inv * (scaled - unit * inner)).astype(BF)

        def place_of(j, x2):
            return (x2 * NY + mod(y + j, NY)) * (PART // 2)

        class Lanes:
            def __init__(self, q, grad):
                self.q, self.grad = q, grad
                for name in ("T", "sibr", "yst", "yr", "R"):
                    setattr(self, name, getattr(r, name + str(q)))

            def block(self, half, zh, js):
                pairs = [(j, x2) for j in js for x2 in range(XH)]
                left = []
                for j, x2 in pairs:
                    first = half * HALF + (x2 * NY + mod(y + j, NY)) * PART + zh * 48
                    left += [r.xnT[rows(first + zq * 96, 48, 48), :] for zq in range(2)]
                out = dot(jnp.concatenate(left, axis=0), self.grad[...]).astype(BF)
                for i, (j, x2) in enumerate(pairs):
                    at = rows(half * (HALF // 2) + place_of(j, x2), 96, 96)
                    self.T[zh, at, :] = out[i * 96 : i * 96 + 96]

            def to_sibling(self, zh, js):
                self.block(1 - c, zh, js)
                for j in js:
                    for x2 in range(XH):
                        src = self.T.at[zh, rows((1 - c) * (HALF // 2) + place_of(j, x2), 96, 96)]
                        dst = self.sibr.at[zh, rows(place_of(j, x2), 96, 96)]
                        send(src, dst, r.ts_s.at[self.q], r.ts_r.at[self.q, j, zh], sib)

            def chunks_out(self, zh, js):
                ys = r.y_s.at[self.q]
                for j in js:
                    take(self.sibr.at[zh, 0:PART], r.ts_r.at[self.q, j, zh])
                    for x2 in range(XH):
                        mine = self.T[zh, rows(c * (HALF // 2) + place_of(j, x2), 96, 96), :]
                        theirs = self.sibr[zh, rows(place_of(j, x2), 96, 96), :]
                        src = self.yst.at[zh, j, x2]
                        src[...] = (mine.astype(F32) + theirs.astype(F32)).astype(BF)

                        @pl.when(c == 0)
                        def _():
                            target = device(0, x2, mod(y + j, NY), z, xh)
                            send(src, self.yr.at[zh, j, 0], ys, r.y_r.at[self.q, 0, zh], target)

                        @pl.when(c == 1)
                        def _():
                            dst, arrive = self.yr.at[zh, j, x2], r.y_r.at[self.q, x2, zh]
                            if j:
                                send(src, dst, ys, arrive, device(1, xh, mod(y + j, NY), z, 1))
                            else:
                                pltpu.make_async_copy(src, dst, arrive).start()

            def drain(self):
                take(self.sibr, r.ts_s.at[self.q])
                take(self.yst.at[:, 0:3], r.y_s.at[self.q])

                @pl.when(c == 0)
                def _():
                    take(self.yst.at[:, 3], r.y_s.at[self.q])

        a, b = Lanes(0, r.dv), Lanes(1, r.dqk)
        near, rest = (2, 1), (3, 0)
        for t in range(4):
            scores_back(t)
        unnorm(q_l, gain_q, r.dq[...])
        unnorm(k_l, gain_k, r.dk[...])
        b.to_sibling(0, near)
        b.to_sibling(0, rest)
        b.block(c, 0, near)
        b.block(c, 0, rest)
        b.chunks_out(0, near)
        b.to_sibling(1, near)
        b.chunks_out(0, rest)
        b.to_sibling(1, rest)
        b.block(c, 1, near)
        b.block(c, 1, rest)
        b.chunks_out(1, near + rest)
        dv = dot(r.pb[0], r.d_att[0:TILE, :])
        for t in range(1, 4):
            dv = dv + dot(r.pb[t], r.d_att[t * TILE : t * TILE + TILE, :])
        r.dv[...] = dv.astype(BF)
        a.to_sibling(0, near)
        a.to_sibling(0, rest)
        a.block(c, 0, near)
        a.block(c, 0, rest)
        a.chunks_out(0, near)
        a.to_sibling(1, near)
        a.to_sibling(1, rest)
        a.chunks_out(0, rest)
        a.block(c, 1, near)
        a.block(c, 1, rest)
        a.chunks_out(1, near + rest)
        generator()

        @pl.when(c == 1)
        def _():
            for q in (1, 0):
                for zh in range(2):
                    for x2 in range(XH):
                        deliver(q, zh, x2, 1, x2, h)
            for R, fs in ((r.R0, r.f_s.at[0]), (r.R1, r.f_s.at[1])):
                take(R, fs)
                take(R.at[0:15], fs)

        a.drain()
        b.drain()
        take(r.cot.at[0 : 15 * 32], r.d_s)

    take(r.n1r.at[0:7], r.n1_s)
    take(r.w0s, r.w0_s)
    take(NL.at[0 : 7 * 32], r.nz_s)
    take(NL.at[0 : 3 * 256], r.nx_s)
    for k in range(3):
        if k == 2:
            left(2)
        take(W.at[k, 0 : 7 * 2 * PART], r.w_s)

    take(r.p1r.at[0:15], r.p1_s)
    take(r.pmine, r.x_s)
    take(r.gr.at[0:7], r.g_s)
    take(r.gr, r.g_r)
    for b in range(SAMPLES):
        r.gen[b * 4 : b * 4 + 4, :] = r.gr[b, 0:4, :]
    take(r.R0, r.f_r.at[0])
    r.Rf[:, :, v_l] = r.R0[...].astype(F32)
    take(r.R1, r.f_r.at[1])
    r.Rf[:, :, qk_l] = r.R1[...].astype(F32)
    for i in range(12):
        r.grad[i * HEADS : i * HEADS + HEADS, :] = r.Rf[:, i, :].astype(BF)


def on_device(latents, noise, steps_t, w_in, norm_gain, w_qkv, q_gain, k_gain, w_out):
    gen, grads = pl.pallas_call(
        mega_kernel,
        out_shape=(
            jax.ShapeDtypeStruct((SAMPLES * 4, 128), F32),
            jax.ShapeDtypeStruct((12 * HEADS, TRIPLE), BF),
        ),
        in_specs=[HB, HB, SM, HB, HB, HB, HB, HB, HB],
        out_specs=(VM, VM),
        scratch_shapes=[pltpu.VMEM(*spec) for spec in SCRATCH.values()]
        + [DMA if n is None else DMA(n if isinstance(n, tuple) else (n,)) for n in SEMS.values()],
        compiler_params=pltpu.CompilerParams(
            collective_id=0, has_side_effects=True, vmem_limit_bytes=58 * 1024 * 1024
        ),
        name="distill_step",
    )(latents, noise, steps_t, w_in, norm_gain, w_qkv, q_gain, k_gain, w_out.transpose(0, 2, 1))
    grads = grads.astype(F32).reshape(12, HEADS, TRIPLE).transpose(1, 0, 2)
    return gen[:, :CH].reshape(SAMPLES, 4, CH), grads


def solution(mesh):
    return jax.shard_map(
        on_device,
        mesh=mesh,
        in_specs=(
            P(None, ("grp", "mp"), None),
            P(None, ("grp", "mp"), None),
            P(),
            P("grp", None, None),
            P("grp", None),
            P("grp", None, "mp", None),
            P("grp", None, None),
            P("grp", None, None),
            P("grp", None, None),
        ),
        out_specs=(P(None, ("grp", "mp"), None), P(None, ("grp", "mp"), None)),
        check_vma=False,
    )
```

```python
import functools
import math

import jax
import jax.numpy as jnp
from jax import lax
from jax.experimental import pallas as pl
from jax.experimental.pallas import tpu as pltpu
from jax.sharding import PartitionSpec as P

MESH = pl.DeviceIdType.MESH
XH, NY, NZ, NC = 2, 4, 8, 2
HEADS, SAMPLES = XH * NZ, NY * NC
D, HD, CH, LEN = 3072, 128, 64, 1024
TRIPLE = 3 * HD
BF, F32 = jnp.bfloat16, jnp.float32


def place():
    m = lax.axis_index("mp")
    return (
        lax.axis_index("grp"),
        m // (NY * NZ * NC),
        (m // (NZ * NC)) % NY,
        (m // NC) % NZ,
        m % NC,
    )


def device(g, xh, y, z, c):
    return (g, ((xh * NY + y) * NZ + z) * NC + c)


def mod(a, n):
    return lax.rem(a, n)


def rows(start, size, step):
    return pl.ds(pl.multiple_of(start, step), size)


def send(src, dst, ssem, rsem, target):
    copy = pltpu.make_async_remote_copy(
        src_ref=src, dst_ref=dst, send_sem=ssem, recv_sem=rsem, device_id=target, device_id_type=MESH
    )
    copy.start()


def take(ref, sem):
    pltpu.make_async_copy(ref, ref, sem).wait()


def greet(barrier, target):
    pl.semaphore_signal(barrier, inc=1, device_id=target, device_id_type=MESH)


Z_ORDER = (0, 1, 7, 2, 6, 3, 5, 4)


DMA = pltpu.SemaphoreType.DMA
VM = pl.BlockSpec(memory_space=pltpu.VMEM)
SM = pl.BlockSpec(memory_space=pltpu.SMEM)
HB = pl.BlockSpec(memory_space=pl.ANY)
HALF, PART = D // 2, 192
TILE = 256
SCALE = 1.0 / math.sqrt(HD)
FAR_FIRST = (4, 3, 5, 2, 6, 1, 7, 0)


def dot(a, b, ca=1, cb=0):
    return lax.dot_general(a, b, (((ca,), (cb,)), ((), ())), preferred_element_type=F32)


SCRATCH = dict(
    lat=((SAMPLES, 4, CH), BF),
    noise=((SAMPLES, 4, CH), BF),
    gain=((1, D), F32),
    q_gain=((1, HEADS, HD), F32),
    k_gain=((1, HEADS, HD), F32),
    w_own=((HEADS, 24, TRIPLE), BF),
    w_in=((CH, D), BF),
    w_outT=((CH, HD), BF),
    W=((3, D, HD), BF),
    NL=((LEN, 128), BF),
    w0s=((NZ, 32, TRIPLE), BF),
    w0r=((NZ, 32, TRIPLE), BF),
    w1s=((3, NZ, 48, HD), BF),
    nst=((SAMPLES, 16, 128), BF),
    n1r=((SAMPLES, 16, 128), BF),
    nsf=((SAMPLES, 16, 128), F32),
    n1f=((32, 128), F32),
    temb=((8, D), F32),
    xf=((128, D), F32),
    xn=((LEN, D), BF),
    xnT=((D, LEN), BF),
    qkv=((LEN, TRIPLE), F32),
    qn=((LEN, HD), BF),
    kn=((LEN, HD), BF),
    v=((LEN, HD), BF),
    knT=((HD, LEN), BF),
    vT=((HD, LEN), BF),
    p32=((4, LEN, TILE), F32),
    pb=((4, LEN, TILE), BF),
    pp=((LEN // 2, 128), BF),
    p1r=((HEADS, 32, 128), BF),
    dch=((32, 128), BF),
    cot=((LEN // 2, 128), BF),
    pmine=((32, 128), F32),
    pother=((32, 128), F32),
    gs=((SAMPLES, 8, 128), F32),
    d_att=((LEN, HD), BF),
    dq=((LEN, HD), F32),
    dk=((LEN, HD), F32),
    dqk=((LEN, 2 * HD), BF),
    dv=((LEN, HD), BF),
    gr=((SAMPLES, 8, 128), F32),
    Rf=((HEADS, 16, TRIPLE), F32),
    **{
        name + str(q): (shape[:-1] + (n,), kind)
        for q, n in ((0, HD), (1, 2 * HD))
        for name, shape, kind in (
            ("T", (2, HALF, 0), BF),
            ("sibr", (2, HALF // 2, 0), BF),
            ("yst", (2, NY, XH, PART // 2, 0), BF),
            ("yr", (2, NY, XH, PART // 2, 0), BF),
            ("fin", (PART // 2, 0), F32),
            ("st", (2, XH, 8, 16, 0), BF),
            ("R", (HEADS, 16, 0), BF),
        )
    },
)
SEMS = dict(
    n1_s=None, n1_r=None, nz_s=None, nz_r=None, nx_s=None, nx_r=None, w0_s=None, w0_r=None, w_s=None,
    w1_s=3, w1_r=3, wa_r=3, wb_r=3, wr_r=3, sb_r=(3, 2), p1_s=None, p1_r=None, d_s=None, d_r=XH,
    x_s=None, x_r=None, g_s=None, g_r=None, ts_s=2, ts_r=(2, NY, 2), y_s=2,
    y_r=(2, XH, 2), f_s=2, f_r=2, in_r=8,
)
INPUTS = (
    "lat_hbm", "noise_hbm", "steps", "w_in_hbm", "gain_hbm", "w_qkv", "q_gain_hbm", "k_gain_hbm", "w_out"
)


class Refs:
    pass


def mega_kernel(*args):
    r = Refs()
    names = INPUTS + ("gen", "grad") + tuple(SCRATCH) + tuple(SEMS)
    for name, ref in zip(names, args, strict=True):
        setattr(r, name, ref)
    g, xh, y, z, c = place()
    h, me_b, X = xh * NZ + z, y * NC + c, xh * 2 + g
    fake, cross = g == 1, xh != c
    W, NL = r.W, r.NL

    def yc(dy, dc):
        return mod(y + dy, NY), mod(c + dc, NC)

    def zline(dz):
        return device(g, xh, y, mod(z + dz, NZ), c)

    def xline(dx):
        X2 = mod(X + dx, 4)
        return device(mod(X2, 2), X2 // 2, y, z, c)

    barrier = pltpu.get_barrier_semaphore()
    for dy in range(NY):
        for dc in range(NC):
            if dy or dc:
                y2, c2 = yc(dy, dc)
                greet(barrier, device(g, xh, y2, z, c2))
    for dz in range(1, NZ):
        greet(barrier, zline(dz))
    for dx in range(1, 4):
        greet(barrier, xline(dx))

    @pl.when(cross)
    def _():
        for dz in range(NZ):
            greet(barrier, device(g, c, y, mod(z + dz, NZ), xh))

    loads = (
        pltpu.make_async_copy(r.w_qkv.at[0], r.w_own, r.in_r.at[0]),
        pltpu.make_async_copy(r.w_in_hbm.at[0], r.w_in, r.in_r.at[1]),
        pltpu.make_async_copy(
            r.w_out.at[0, :, pl.ds(pl.multiple_of(h * HD, HD), HD)], r.w_outT, r.in_r.at[2]
        ),
        pltpu.make_async_copy(r.lat_hbm, r.lat, r.in_r.at[3]),
        pltpu.make_async_copy(r.noise_hbm, r.noise, r.in_r.at[4]),
        pltpu.make_async_copy(r.gain_hbm, r.gain, r.in_r.at[5]),
        pltpu.make_async_copy(r.q_gain_hbm, r.q_gain, r.in_r.at[6]),
        pltpu.make_async_copy(r.k_gain_hbm, r.k_gain, r.in_r.at[7]),
    )
    for load in loads:
        load.start()

    loads[0].wait()
    for j in range(NZ):
        r.w0s[j, 0:24, :] = r.w_own[(1 - c) * NZ + j]
        r.w0s[j, 24:32, :] = jnp.zeros((8, TRIPLE), BF)

    loads[3].wait()
    loads[4].wait()
    rows8 = lax.broadcasted_iota(jnp.int32, (SAMPLES, 128), 0)
    ang = jnp.zeros((SAMPLES, 128), F32)
    for b in range(SAMPLES):
        ang = jnp.where(rows8 == b, r.steps[b].astype(F32), ang)
    ang = 0.5 * math.pi / 1000.0 * ang
    alpha, sigma = jnp.cos(ang), jnp.sin(ang)
    r.nsf[...] = jnp.zeros_like(r.nsf)
    r.gs[...] = jnp.zeros_like(r.gs)
    for b in range(SAMPLES):
        latent = r.lat[b].astype(F32)
        noisy = alpha[b : b + 1, 0:CH] * latent + sigma[b : b + 1, 0:CH] * r.noise[b].astype(F32)
        r.nsf[b, 0:4, 0:CH] = noisy
        r.nsf[b, 0:4, CH:128] = latent
    r.nst[...] = r.nsf[...].astype(BF)

    pl.semaphore_wait(barrier, 7 + 7 + 3 + jnp.where(cross, NZ, 0))

    sib = device(g, xh, y, z, 1 - c)
    send(r.w0s, r.w0r, r.w0_s, r.w0_r, sib)
    for dy in range(NY):
        for dc in range(NC):
            y2, c2 = yc(dy, dc)
            src = r.nst.at[y2 * NC + c2]
            if dy or dc:
                send(src, r.n1r.at[me_b], r.n1_s, r.n1_r, device(g, xh, y2, z, c2))
            else:
                pltpu.make_async_copy(src, r.n1r.at[me_b], r.n1_r).start()

    take(r.w0r, r.w0_r)
    for j in range(NZ):
        mine = r.w_own[c * NZ + j].astype(F32)
        theirs = r.w0r[j, 0:24, :].astype(F32)
        low = jnp.where(c == 0, mine, theirs)
        high = jnp.where(c == 0, theirs, mine)
        both = jnp.concatenate([low, high], axis=0).astype(BF)
        for k in range(3):
            r.w1s[k, j] = both[:, k * HD : k * HD + HD]

    def to_heads(k):
        for dz in Z_ORDER:
            z2 = mod(z + dz, NZ)
            src, dst = r.w1s.at[k, z2], W.at[k, rows(((xh * NY + y) * NZ + z) * 48, 48, 48)]
            if dz:
                send(src, dst, r.w1_s.at[k], r.w1_r.at[k], device(g, c, y, z2, xh))
            else:

                @pl.when(cross)
                def _():
                    send(src, dst, r.w1_s.at[k], r.w1_r.at[k], device(g, c, y, z2, xh))

                @pl.when(jnp.logical_not(cross))
                def _():
                    pltpu.make_async_copy(src, dst, r.w1_r.at[k]).start()

    def left(k):
        take(W.at[k, 0 : 7 * 48], r.w1_s.at[k])

        @pl.when(cross)
        def _():
            take(W.at[k, 0:48], r.w1_s.at[k])

    to_heads(0)

    take(r.n1r, r.n1_r)
    for j in range(SAMPLES):
        r.n1f[j * 4 : j * 4 + 4, :] = r.n1r[j, 0:4, :].astype(F32)
    own_n = rows((X * NZ + z) * 32, 32, 32)
    NL[own_n, :] = r.n1f[...].astype(BF)
    for dz in FAR_FIRST[:7]:
        send(NL.at[own_n], NL.at[own_n], r.nz_s, r.nz_r, zline(dz))

    up, down = device(g, xh, mod(y + 1, NY), z, c), device(g, xh, mod(y + 3, NY), z, c)

    def chunk(dy, k, off=0, size=2 * PART):
        return W.at[k, rows((c * NY + mod(y + dy, NY)) * 2 * PART + off, size, PART)]

    def pass_on(ref, rsem, target):
        send(ref, ref, r.w_s, rsem, target)

    def relay_own(k):
        ref = chunk(0, k)
        take(ref, r.w1_r.at[k])
        pass_on(ref, r.wa_r.at[k], up)
        pass_on(ref, r.wb_r.at[k], down)
        if k:
            pass_on(ref, r.wr_r.at[k], device(g, xh, mod(y + 2, NY), z, c))
        pass_on(ref, r.sb_r.at[k, 0], sib)

    def relay_near(k):
        take(chunk(3, k), r.wa_r.at[k])
        if k == 0:
            pass_on(chunk(3, k, 0, PART), r.wr_r.at[k], up)
        pass_on(chunk(3, k), r.sb_r.at[k, 0], sib)
        take(chunk(1, k), r.wb_r.at[k])
        if k == 0:
            pass_on(chunk(1, k, PART, PART), r.wr_r.at[k], down)
        pass_on(chunk(1, k), r.sb_r.at[k, 0], sib)

    def relay_far(k):
        take(chunk(2, k), r.wr_r.at[k])
        pass_on(chunk(2, k), r.sb_r.at[k, 1], sib)

    t_value = r.steps[me_b].astype(F32)
    index = lax.broadcasted_iota(jnp.int32, (1, D // 2), 1).astype(F32)
    phase = t_value * jnp.exp(-math.log(10000.0) * index / (D // 2))
    r.temb[0:1, 0 : D // 2] = jnp.sin(phase)
    r.temb[0:1, D // 2 :] = jnp.cos(phase)

    left(0)
    to_heads(1)
    relay_own(0)
    take(NL.at[0 : 7 * 32], r.nz_r)
    own_x = rows(X * 256, 256, 256)
    for dx in range(1, 4):
        send(NL.at[own_x], NL.at[own_x], r.nx_s, r.nx_r, xline(dx))
    left(1)
    to_heads(2)
    for i in (1, 5, 6, 7):
        loads[i].wait()

    def embed(tile):
        at = rows(tile * 128, 128, 128)
        noisy = NL[at, :][:, 0:CH]
        total = jnp.zeros((128, 128), F32)
        for k in range(D // 512):
            part = dot(noisy, r.w_in[:, k * 512 : k * 512 + 512]) + r.temb[0:1, k * 512 : k * 512 + 512]
            r.xf[:, k * 512 : k * 512 + 512] = part
            sq = part * part
            for i in range(4):
                total = total + sq[:, i * 128 : i * 128 + 128]
        inv = lax.rsqrt(jnp.sum(total, axis=1, keepdims=True) * (1.0 / D) + 1e-06)
        for k in range(D // 512):
            cols = slice(k * 512, k * 512 + 512)
            done = (r.xf[:, cols] * inv * r.gain[0:1, cols]).astype(BF)
            r.xn[at, cols] = done

            @pl.when(fake)
            def _():
                r.xnT[cols, at] = done.T

    steps = {
        0: [(relay_own, 1)], 1: [(relay_near, 0)], 2: [(relay_own, 2), (relay_far, 0)],
        4: [(relay_near, 1)], 5: [(relay_far, 1)], 6: [(relay_near, 2)],
    }
    for i in range(8):
        if i == 2:
            take(NL.at[0 : 3 * 256], r.nx_r)
        embed(mod(X * 2 + i, 8))
        for step, k in steps.get(i, ()):
            step(k)

    def project(half, first, lanes, ks):
        cols = rows(half * HALF, HALF, HALF)
        weight = jnp.concatenate([W[k, cols, :] for k in ks], axis=1)
        for i in range(4):
            at = slice(i * TILE, i * TILE + TILE)
            part = dot(r.xn[at, cols], weight)
            r.qkv[at, lanes] = part if first else r.qkv[at, lanes] + part

    qk_l, v_l = slice(0, 2 * HD), slice(2 * HD, TRIPLE)
    project(c, True, qk_l, (0, 1))
    for k in range(2):
        take(W.at[k, 0 : 6 * PART], r.sb_r.at[k, 0])
        take(W.at[k, 0 : 2 * PART], r.sb_r.at[k, 1])
    project(1 - c, False, qk_l, (0, 1))
    relay_far(2)

    gain_q, gain_k = r.q_gain[0, pl.ds(h, 1), :], r.k_gain[0, pl.ds(h, 1), :]

    def normed(lanes):
        raw = r.qkv[:, lanes]
        inv = lax.rsqrt(jnp.mean(raw * raw, axis=-1, keepdims=True) + 1e-06)
        return raw, inv

    q_l, k_l = slice(0, HD), slice(HD, 2 * HD)
    raw, inv = normed(q_l)
    r.qn[...] = (raw * inv * gain_q).astype(BF)
    raw, inv = normed(k_l)
    k_norm = (raw * inv * gain_k).astype(BF)
    r.kn[...] = k_norm
    r.knT[...] = k_norm.T
    for t in range(4):
        at = slice(t * TILE, t * TILE + TILE)
        scores = dot(r.kn[...], r.qn[at, :], 1, 1)
        expo = jnp.exp2(scores * (SCALE * math.log2(math.e)))
        probs = expo * (1.0 / jnp.sum(expo, axis=0, keepdims=True))
        r.p32[t] = probs
        r.pb[t] = probs.astype(BF)

    project(c, True, v_l, (2,))

    def project_v(dy):
        cols = rows(((1 - c) * NY + mod(y + dy, NY)) * 2 * PART, 2 * PART, 2 * PART)
        for i in range(4):
            at = slice(i * TILE, i * TILE + TILE)
            r.qkv[at, v_l] += dot(r.xn[at, cols], W[2, cols, :])

    take(W.at[2, 0 : 6 * PART], r.sb_r.at[2, 0])
    for dy in (0, 3, 1):
        project_v(dy)
    take(W.at[2, 0 : 2 * PART], r.sb_r.at[2, 1])
    project_v(2)
    value = r.qkv[:, v_l].astype(BF)
    r.v[...] = value
    r.vT[...] = value.T
    loads[2].wait()

    halves = []
    for t in range(4):
        attended = dot(r.vT[...], r.pb[t]).astype(BF)
        halves.append(dot(r.w_outT[...], attended).T)
        if t % 2 == 1:
            x2 = t // 2
            r.pp[x2 * 256 : x2 * 256 + 256, :] = jnp.concatenate(halves, axis=1).astype(BF)
            halves = []
            for dz in FAR_FIRST:
                z2 = mod(z + dz, NZ)
                src, dst = r.pp.at[rows((x2 * NZ + z2) * 32, 32, 32)], r.p1r.at[h]
                if dz:
                    send(src, dst, r.p1_s, r.p1_r, device(g, x2, y, z2, c))
                else:

                    @pl.when(xh == x2)
                    def _():
                        pltpu.make_async_copy(src, dst, r.p1_r).start()

                    @pl.when(xh != x2)
                    def _():
                        send(src, dst, r.p1_s, r.p1_r, device(g, x2, y, z2, c))

    take(r.p1r, r.p1_r)
    pred = jnp.sum(r.p1r[...].astype(F32), axis=0)
    r.pmine[...] = pred

    @pl.when(fake)
    def _():
        lat0 = NL[rows((xh * 2 * NZ + z) * 32, 32, 32), :].astype(F32)[:, CH:]
        lat1 = NL[rows(((xh * 2 + 1) * NZ + z) * 32, 32, 32), :].astype(F32)[:, CH:]
        latent = jnp.concatenate([lat0, lat1], axis=1)
        r.dch[...] = ((pred - latent) * (1.0 / SAMPLES)).astype(BF)
        own = rows(h * 32, 32, 32)
        for dx in (1, 0):
            for dz in FAR_FIRST:
                if dx or dz:
                    target = device(g, mod(xh + dx, XH), y, mod(z + dz, NZ), c)
                    send(r.dch, r.cot.at[own], r.d_s, r.d_r.at[xh], target)
        pltpu.make_async_copy(r.dch, r.cot.at[own], r.d_r.at[xh]).start()

    partner = device(1 - g, xh, y, z, c)
    send(r.pmine, r.pother, r.x_s, r.x_r, partner)

    def generator():
        take(r.pother, r.x_r)
        diff = jnp.where(g == 0, r.pother[...] - r.pmine[...], r.pmine[...] - r.pother[...])
        mine = jnp.where(g == 0, diff[:, 0:CH], diff[:, CH:])
        for j in range(SAMPLES):
            r.gs[j, 0:4, 0:CH] = mine[j * 4 : j * 4 + 4, :]
        for dy in range(NY):
            for dc in range(NC):
                y2, c2 = yc(dy, dc)
                src, dst = r.gs.at[y2 * NC + c2], r.gr.at[me_b]
                if dy or dc:
                    send(src, dst, r.g_s, r.g_r, device(g, xh, y2, z, c2))
                else:
                    pltpu.make_async_copy(src, dst, r.g_r).start()

    def deliver(q, zh, slot, net, x2, head):
        yr, fin, st, R = (getattr(r, name + str(q)) for name in ("yr", "fin", "st", "R"))
        take(yr.at[zh, :, slot], r.y_r.at[q, slot, zh])
        fin[...] = jnp.sum(yr[zh, :, slot].astype(F32), axis=0)
        for i in range(8):
            st[zh, slot, i, 0:12, :] = fin[i * 12 : i * 12 + 12, :].astype(BF)
        fs, fr = r.f_s.at[q], r.f_r.at[q]
        for e in (3, 2, 1, 0):
            zq, zr = mod(z // 4 + e // 2, 2), mod(z + e, 2)
            z2 = zq * 4 + zh * 2 + zr
            for c2 in range(NC):
                src, dst = st.at[zh, slot, (zq * 2 + zr) * NC + c2], R.at[head]
                target = device(net, x2, y, z2, c2)
                if e:
                    send(src, dst, fs, fr, target)
                else:
                    me = (x2 == xh) & (c2 == c) & (z2 == z)

                    @pl.when(me)
                    def _():
                        pltpu.make_async_copy(src, dst, fr).start()

                    @pl.when(jnp.logical_not(me))
                    def _():
                        send(src, dst, fs, fr, target)


    @pl.when(jnp.logical_not(fake))
    def _():
        generator()
        for q in (1, 0):
            for zh in range(2):
                deliver(q, zh, 0, 0, xh, c * NZ + z)
        for q in range(2):
            take(getattr(r, f"R{q}").at[0:15], r.f_s.at[q])

    @pl.when(fake)
    def _():
        def scores_back(i):
            x2 = mod(xh + i // 2, XH)
            if i % 2 == 0:
                take(r.cot.at[0:256], r.d_r.at[x2])
            t = x2 * 2 + i % 2
            at = rows(t * TILE, TILE, TILE)
            cot = r.cot[rows(x2 * 256, 256, 256), (i % 2) * CH : (i % 2) * CH + CH]
            r.d_att[at, :] = dot(cot, r.w_outT[...]).astype(BF)
            d_probs = dot(r.v[...], r.d_att[at, :], 1, 1)
            probs = r.p32[t]
            mean = jnp.sum(probs * d_probs, axis=0, keepdims=True)
            d_score = (probs * (d_probs - mean)).astype(BF)
            dk = dot(d_score, r.qn[at, :])
            if i:
                r.dk[...] += dk
            else:
                r.dk[...] = dk
            r.dq[at, :] = dot(r.knT[...], d_score).T

        def unnorm(lanes, gain, grad):
            raw, inv = normed(lanes)
            scaled = grad * SCALE * gain
            unit = raw * inv
            inner = jnp.mean(unit * scaled, axis=-1, keepdims=True)
            r.dqk[:, lanes] = (inv * (scaled - unit * inner)).astype(BF)

        def place_of(j, x2):
            return (x2 * NY + mod(y + j, NY)) * (PART // 2)

        class Lanes:
            def __init__(self, q, grad):
                self.q, self.grad = q, grad
                for name in ("T", "sibr", "yst", "yr", "R"):
                    setattr(self, name, getattr(r, name + str(q)))

            def block(self, half, zh, js):
                pairs = [(j, x2) for j in js for x2 in range(XH)]
                left = []
                for j, x2 in pairs:
                    first = half * HALF + (x2 * NY + mod(y + j, NY)) * PART + zh * 48
                    left += [r.xnT[rows(first + zq * 96, 48, 48), :] for zq in range(2)]
                out = dot(jnp.concatenate(left, axis=0), self.grad[...]).astype(BF)
                for i, (j, x2) in enumerate(pairs):
                    at = rows(half * (HALF // 2) + place_of(j, x2), 96, 96)
                    self.T[zh, at, :] = out[i * 96 : i * 96 + 96]

            def to_sibling(self, zh, js):
                self.block(1 - c, zh, js)
                for j in js:
                    for x2 in range(XH):
                        src = self.T.at[zh, rows((1 - c) * (HALF // 2) + place_of(j, x2), 96, 96)]
                        dst = self.sibr.at[zh, rows(place_of(j, x2), 96, 96)]
                        send(src, dst, r.ts_s.at[self.q], r.ts_r.at[self.q, j, zh], sib)

            def chunks_out(self, zh, js):
                ys = r.y_s.at[self.q]
                for j in js:
                    take(self.sibr.at[zh, 0:PART], r.ts_r.at[self.q, j, zh])
                    for x2 in range(XH):
                        mine = self.T[zh, rows(c * (HALF // 2) + place_of(j, x2), 96, 96), :]
                        theirs = self.sibr[zh, rows(place_of(j, x2), 96, 96), :]
                        src = self.yst.at[zh, j, x2]
                        src[...] = (mine.astype(F32) + theirs.astype(F32)).astype(BF)

                        @pl.when(c == 0)
                        def _():
                            target = device(0, x2, mod(y + j, NY), z, xh)
                            send(src, self.yr.at[zh, j, 0], ys, r.y_r.at[self.q, 0, zh], target)

                        @pl.when(c == 1)
                        def _():
                            dst, arrive = self.yr.at[zh, j, x2], r.y_r.at[self.q, x2, zh]
                            if j:
                                send(src, dst, ys, arrive, device(1, xh, mod(y + j, NY), z, 1))
                            else:
                                pltpu.make_async_copy(src, dst, arrive).start()

            def drain(self):
                take(self.sibr, r.ts_s.at[self.q])
                take(self.yst.at[:, 0:3], r.y_s.at[self.q])

                @pl.when(c == 0)
                def _():
                    take(self.yst.at[:, 3], r.y_s.at[self.q])

        a, b = Lanes(0, r.dv), Lanes(1, r.dqk)
        near, rest = (2, 1), (3, 0)
        for t in range(4):
            scores_back(t)
        unnorm(q_l, gain_q, r.dq[...])
        unnorm(k_l, gain_k, r.dk[...])
        b.to_sibling(0, near)
        b.to_sibling(0, rest)
        b.block(c, 0, near)
        b.block(c, 0, rest)
        b.chunks_out(0, near)
        b.to_sibling(1, near)
        b.chunks_out(0, rest)
        b.to_sibling(1, rest)
        b.block(c, 1, near)
        b.block(c, 1, rest)
        b.chunks_out(1, near + rest)
        dv = dot(r.pb[0], r.d_att[0:TILE, :])
        for t in range(1, 4):
            dv = dv + dot(r.pb[t], r.d_att[t * TILE : t * TILE + TILE, :])
        r.dv[...] = dv.astype(BF)
        a.to_sibling(0, near)
        a.to_sibling(0, rest)
        a.block(c, 0, near)
        a.block(c, 0, rest)
        a.chunks_out(0, near)
        a.to_sibling(1, near)
        a.to_sibling(1, rest)
        a.chunks_out(0, rest)
        a.block(c, 1, near)
        a.block(c, 1, rest)
        a.chunks_out(1, near + rest)
        generator()

        @pl.when(c == 1)
        def _():
            for q in (1, 0):
                for zh in range(2):
                    for x2 in range(XH):
                        deliver(q, zh, x2, 1, x2, h)
            for R, fs in ((r.R0, r.f_s.at[0]), (r.R1, r.f_s.at[1])):
                take(R, fs)
                take(R.at[0:15], fs)

        a.drain()
        b.drain()
        take(r.cot.at[0 : 15 * 32], r.d_s)

    take(r.n1r.at[0:7], r.n1_s)
    take(r.w0s, r.w0_s)
    take(NL.at[0 : 7 * 32], r.nz_s)
    take(NL.at[0 : 3 * 256], r.nx_s)
    for k in range(3):
        if k == 2:
            left(2)
        take(W.at[k, 0 : 7 * 2 * PART], r.w_s)

    take(r.p1r.at[0:15], r.p1_s)
    take(r.pmine, r.x_s)
    take(r.gr.at[0:7], r.g_s)
    take(r.gr, r.g_r)
    for b in range(SAMPLES):
        r.gen[b * 4 : b * 4 + 4, :] = r.gr[b, 0:4, :]
    take(r.R0, r.f_r.at[0])
    r.Rf[:, :, v_l] = r.R0[...].astype(F32)
    take(r.R1, r.f_r.at[1])
    r.Rf[:, :, qk_l] = r.R1[...].astype(F32)
    for i in range(12):
        r.grad[i * HEADS : i * HEADS + HEADS, :] = r.Rf[:, i, :].astype(BF)


def on_device(latents, noise, steps_t, w_in, norm_gain, w_qkv, q_gain, k_gain, w_out):
    gen, grads = pl.pallas_call(
        mega_kernel,
        out_shape=(
            jax.ShapeDtypeStruct((SAMPLES * 4, 128), F32),
            jax.ShapeDtypeStruct((12 * HEADS, TRIPLE), BF),
        ),
        in_specs=[HB, HB, SM, HB, HB, HB, HB, HB, HB],
        out_specs=(VM, VM),
        scratch_shapes=[pltpu.VMEM(*spec) for spec in SCRATCH.values()]
        + [DMA if n is None else DMA(n if isinstance(n, tuple) else (n,)) for n in SEMS.values()],
        compiler_params=pltpu.CompilerParams(
            collective_id=0, has_side_effects=True, vmem_limit_bytes=58 * 1024 * 1024
        ),
        name="distill_step",
    )(latents, noise, steps_t, w_in, norm_gain, w_qkv, q_gain, k_gain, w_out.transpose(0, 2, 1))
    grads = grads.astype(F32).reshape(12, HEADS, TRIPLE).transpose(1, 0, 2)
    return gen[:, :CH].reshape(SAMPLES, 4, CH), grads


def solution(mesh):
    return jax.shard_map(
        on_device,
        mesh=mesh,
        in_specs=(
            P(None, ("grp", "mp"), None),
            P(None, ("grp", "mp"), None),
            P(),
            P("grp", None, None),
            P("grp", None),
            P("grp", None, "mp", None),
            P("grp", None, None),
            P("grp", None, None),
            P("grp", None, None),
        ),
        out_specs=(P(None, ("grp", "mp"), None), P(None, ("grp", "mp"), None)),
        check_vma=False,
    )
```

```python
import functools
import math

import jax
import jax.numpy as jnp
from jax import lax
from jax.experimental import pallas as pl
from jax.experimental.pallas import tpu as pltpu
from jax.sharding import PartitionSpec as P

MESH = pl.DeviceIdType.MESH
XH, NY, NZ, NC = 2, 4, 8, 2
HEADS, SAMPLES = XH * NZ, NY * NC
D, HD, CH, LEN = 3072, 128, 64, 1024
TRIPLE = 3 * HD
BF, F32 = jnp.bfloat16, jnp.float32


def place():
    m = lax.axis_index("mp")
    return (
        lax.axis_index("grp"),
        m // (NY * NZ * NC),
        (m // (NZ * NC)) % NY,
        (m // NC) % NZ,
        m % NC,
    )


def device(g, xh, y, z, c):
    return (g, ((xh * NY + y) * NZ + z) * NC + c)


def mod(a, n):
    return lax.rem(a, n)


def rows(start, size, step):
    return pl.ds(pl.multiple_of(start, step), size)


def send(src, dst, ssem, rsem, target):
    copy = pltpu.make_async_remote_copy(
        src_ref=src, dst_ref=dst, send_sem=ssem, recv_sem=rsem, device_id=target, device_id_type=MESH
    )
    copy.start()


def take(ref, sem):
    pltpu.make_async_copy(ref, ref, sem).wait()


def greet(barrier, target):
    pl.semaphore_signal(barrier, inc=1, device_id=target, device_id_type=MESH)


Z_ORDER = (0, 1, 7, 2, 6, 3, 5, 4)


DMA = pltpu.SemaphoreType.DMA
VM = pl.BlockSpec(memory_space=pltpu.VMEM)
SM = pl.BlockSpec(memory_space=pltpu.SMEM)
HB = pl.BlockSpec(memory_space=pl.ANY)
HALF, PART = D // 2, 192
TILE = 256
SCALE = 1.0 / math.sqrt(HD)
FAR_FIRST = (4, 3, 5, 2, 6, 1, 7, 0)


def dot(a, b, ca=1, cb=0):
    return lax.dot_general(a, b, (((ca,), (cb,)), ((), ())), preferred_element_type=F32)


SCRATCH = dict(
    lat=((SAMPLES, 4, CH), BF),
    noise=((SAMPLES, 4, CH), BF),
    gain=((1, D), F32),
    q_gain=((1, HEADS, HD), F32),
    k_gain=((1, HEADS, HD), F32),
    w_own=((HEADS, 24, TRIPLE), BF),
    w_in=((CH, D), BF),
    w_outT=((CH, HD), BF),
    W=((3, D, HD), BF),
    NL=((LEN, 128), BF),
    w0s=((NZ, 32, TRIPLE), BF),
    w0r=((NZ, 32, TRIPLE), BF),
    w1s=((3, NZ, 48, HD), BF),
    nst=((SAMPLES, 16, 128), BF),
    n1r=((SAMPLES, 16, 128), BF),
    nsf=((SAMPLES, 16, 128), F32),
    n1f=((32, 128), F32),
    temb=((8, D), F32),
    xf=((128, D), F32),
    xn=((LEN, D), BF),
    xnT=((D, LEN), BF),
    qkv=((LEN, TRIPLE), F32),
    qn=((LEN, HD), BF),
    kn=((LEN, HD), BF),
    v=((LEN, HD), BF),
    knT=((HD, LEN), BF),
    vT=((HD, LEN), BF),
    p32=((4, LEN, TILE), F32),
    pb=((4, LEN, TILE), BF),
    pp=((LEN // 2, 128), BF),
    p1r=((HEADS, 32, 128), BF),
    dch=((32, 128), BF),
    cot=((LEN // 2, 128), BF),
    pmine=((32, 128), F32),
    pother=((32, 128), F32),
    gs=((SAMPLES, 8, 128), F32),
    d_att=((LEN, HD), BF),
    dq=((LEN, HD), F32),
    dk=((LEN, HD), F32),
    dqk=((LEN, 2 * HD), BF),
    dv=((LEN, HD), BF),
    gr=((SAMPLES, 8, 128), F32),
    Rf=((HEADS, 16, TRIPLE), F32),
    **{
        name + str(q): (shape[:-1] + (n,), kind)
        for q, n in ((0, HD), (1, 2 * HD))
        for name, shape, kind in (
            ("T", (2, HALF, 0), BF),
            ("sibr", (2, HALF // 2, 0), BF),
            ("yst", (2, NY, XH, PART // 2, 0), BF),
            ("yr", (2, NY, XH, PART // 2, 0), BF),
            ("fin", (PART // 2, 0), F32),
            ("st", (2, XH, 8, 16, 0), BF),
            ("R", (HEADS, 16, 0), BF),
        )
    },
)
SEMS = dict(
    n1_s=None, n1_r=None, nz_s=None, nz_r=None, nx_s=None, nx_r=None, w0_s=None, w0_r=None, w_s=None,
    w1_s=3, w1_r=3, wa_r=3, wb_r=3, wr_r=3, sb_r=(3, 2), p1_s=None, p1_r=None, d_s=None, d_r=XH,
    x_s=None, x_r=None, g_s=None, g_r=None, ts_s=2, ts_r=(2, NY, 2), y_s=2,
    y_r=(2, XH, 2), f_s=2, f_r=2, in_r=8,
)
INPUTS = (
    "lat_hbm", "noise_hbm", "steps", "w_in_hbm", "gain_hbm", "w_qkv", "q_gain_hbm", "k_gain_hbm", "w_out"
)


class Refs:
    pass


def mega_kernel(*args):
    r = Refs()
    names = INPUTS + ("gen", "grad") + tuple(SCRATCH) + tuple(SEMS)
    for name, ref in zip(names, args, strict=True):
        setattr(r, name, ref)
    g, xh, y, z, c = place()
    h, me_b, X = xh * NZ + z, y * NC + c, xh * 2 + g
    fake, cross = g == 1, xh != c
    W, NL = r.W, r.NL

    def yc(dy, dc):
        return mod(y + dy, NY), mod(c + dc, NC)

    def zline(dz):
        return device(g, xh, y, mod(z + dz, NZ), c)

    def xline(dx):
        X2 = mod(X + dx, 4)
        return device(mod(X2, 2), X2 // 2, y, z, c)

    barrier = pltpu.get_barrier_semaphore()
    for dy in range(NY):
        for dc in range(NC):
            if dy or dc:
                y2, c2 = yc(dy, dc)
                greet(barrier, device(g, xh, y2, z, c2))
    for dz in range(1, NZ):
        greet(barrier, zline(dz))
    for dx in range(1, 4):
        greet(barrier, xline(dx))

    @pl.when(cross)
    def _():
        for dz in range(NZ):
            greet(barrier, device(g, c, y, mod(z + dz, NZ), xh))

    loads = (
        pltpu.make_async_copy(r.w_qkv.at[0], r.w_own, r.in_r.at[0]),
        pltpu.make_async_copy(r.w_in_hbm.at[0], r.w_in, r.in_r.at[1]),
        pltpu.make_async_copy(
            r.w_out.at[0, :, pl.ds(pl.multiple_of(h * HD, HD), HD)], r.w_outT, r.in_r.at[2]
        ),
        pltpu.make_async_copy(r.lat_hbm, r.lat, r.in_r.at[3]),
        pltpu.make_async_copy(r.noise_hbm, r.noise, r.in_r.at[4]),
        pltpu.make_async_copy(r.gain_hbm, r.gain, r.in_r.at[5]),
        pltpu.make_async_copy(r.q_gain_hbm, r.q_gain, r.in_r.at[6]),
        pltpu.make_async_copy(r.k_gain_hbm, r.k_gain, r.in_r.at[7]),
    )
    for load in loads:
        load.start()

    loads[0].wait()
    for j in range(NZ):
        r.w0s[j, 0:24, :] = r.w_own[(1 - c) * NZ + j]
        r.w0s[j, 24:32, :] = jnp.zeros((8, TRIPLE), BF)

    loads[3].wait()
    loads[4].wait()
    rows8 = lax.broadcasted_iota(jnp.int32, (SAMPLES, 128), 0)
    ang = jnp.zeros((SAMPLES, 128), F32)
    for b in range(SAMPLES):
        ang = jnp.where(rows8 == b, r.steps[b].astype(F32), ang)
    ang = 0.5 * math.pi / 1000.0 * ang
    alpha, sigma = jnp.cos(ang), jnp.sin(ang)
    r.nsf[...] = jnp.zeros_like(r.nsf)
    r.gs[...] = jnp.zeros_like(r.gs)
    for b in range(SAMPLES):
        latent = r.lat[b].astype(F32)
        noisy = alpha[b : b + 1, 0:CH] * latent + sigma[b : b + 1, 0:CH] * r.noise[b].astype(F32)
        r.nsf[b, 0:4, 0:CH] = noisy
        r.nsf[b, 0:4, CH:128] = latent
    r.nst[...] = r.nsf[...].astype(BF)

    pl.semaphore_wait(barrier, 7 + 7 + 3 + jnp.where(cross, NZ, 0))

    sib = device(g, xh, y, z, 1 - c)
    send(r.w0s, r.w0r, r.w0_s, r.w0_r, sib)
    for dy in range(NY):
        for dc in range(NC):
            y2, c2 = yc(dy, dc)
            src = r.nst.at[y2 * NC + c2]
            if dy or dc:
                send(src, r.n1r.at[me_b], r.n1_s, r.n1_r, device(g, xh, y2, z, c2))
            else:
                pltpu.make_async_copy(src, r.n1r.at[me_b], r.n1_r).start()

    take(r.w0r, r.w0_r)
    for j in range(NZ):
        mine = r.w_own[c * NZ + j].astype(F32)
        theirs = r.w0r[j, 0:24, :].astype(F32)
        low = jnp.where(c == 0, mine, theirs)
        high = jnp.where(c == 0, theirs, mine)
        both = jnp.concatenate([low, high], axis=0).astype(BF)
        for k in range(3):
            r.w1s[k, j] = both[:, k * HD : k * HD + HD]

    def to_heads(k):
        for dz in FAR_FIRST:
            z2 = mod(z + dz, NZ)
            src, dst = r.w1s.at[k, z2], W.at[k, rows(((xh * NY + y) * NZ + z) * 48, 48, 48)]
            if dz:
                send(src, dst, r.w1_s.at[k], r.w1_r.at[k], device(g, c, y, z2, xh))
            else:

                @pl.when(cross)
                def _():
                    send(src, dst, r.w1_s.at[k], r.w1_r.at[k], device(g, c, y, z2, xh))

                @pl.when(jnp.logical_not(cross))
                def _():
                    pltpu.make_async_copy(src, dst, r.w1_r.at[k]).start()

    def left(k):
        take(W.at[k, 0 : 7 * 48], r.w1_s.at[k])

        @pl.when(cross)
        def _():
            take(W.at[k, 0:48], r.w1_s.at[k])

    to_heads(0)

    take(r.n1r, r.n1_r)
    for j in range(SAMPLES):
        r.n1f[j * 4 : j * 4 + 4, :] = r.n1r[j, 0:4, :].astype(F32)
    own_n = rows((X * NZ + z) * 32, 32, 32)
    NL[own_n, :] = r.n1f[...].astype(BF)
    for dz in FAR_FIRST[:7]:
        send(NL.at[own_n], NL.at[own_n], r.nz_s, r.nz_r, zline(dz))

    up, down = device(g, xh, mod(y + 1, NY), z, c), device(g, xh, mod(y + 3, NY), z, c)

    def chunk(dy, k, off=0, size=2 * PART):
        return W.at[k, rows((c * NY + mod(y + dy, NY)) * 2 * PART + off, size, PART)]

    def pass_on(ref, rsem, target):
        send(ref, ref, r.w_s, rsem, target)

    def relay_own(k):
        ref = chunk(0, k)
        take(ref, r.w1_r.at[k])
        pass_on(ref, r.wa_r.at[k], up)
        pass_on(ref, r.wb_r.at[k], down)
        if k:
            pass_on(ref, r.wr_r.at[k], device(g, xh, mod(y + 2, NY), z, c))
        pass_on(ref, r.sb_r.at[k, 0], sib)

    def relay_near(k):
        take(chunk(3, k), r.wa_r.at[k])
        if k == 0:
            pass_on(chunk(3, k, 0, PART), r.wr_r.at[k], up)
        pass_on(chunk(3, k), r.sb_r.at[k, 0], sib)
        take(chunk(1, k), r.wb_r.at[k])
        if k == 0:
            pass_on(chunk(1, k, PART, PART), r.wr_r.at[k], down)
        pass_on(chunk(1, k), r.sb_r.at[k, 0], sib)

    def relay_far(k):
        take(chunk(2, k), r.wr_r.at[k])
        pass_on(chunk(2, k), r.sb_r.at[k, 1], sib)

    t_value = r.steps[me_b].astype(F32)
    index = lax.broadcasted_iota(jnp.int32, (1, D // 2), 1).astype(F32)
    phase = t_value * jnp.exp(-math.log(10000.0) * index / (D // 2))
    r.temb[0:1, 0 : D // 2] = jnp.sin(phase)
    r.temb[0:1, D // 2 :] = jnp.cos(phase)

    left(0)
    to_heads(1)
    relay_own(0)
    take(NL.at[0 : 7 * 32], r.nz_r)
    own_x = rows(X * 256, 256, 256)
    for dx in (2, 1, 3):
        send(NL.at[own_x], NL.at[own_x], r.nx_s, r.nx_r, xline(dx))
    left(1)
    to_heads(2)
    for i in (1, 5, 6, 7):
        loads[i].wait()

    def embed(tile):
        at = rows(tile * 128, 128, 128)
        noisy = NL[at, :][:, 0:CH]
        total = jnp.zeros((128, 128), F32)
        for k in range(D // 512):
            part = dot(noisy, r.w_in[:, k * 512 : k * 512 + 512]) + r.temb[0:1, k * 512 : k * 512 + 512]
            r.xf[:, k * 512 : k * 512 + 512] = part
            sq = part * part
            for i in range(4):
                total = total + sq[:, i * 128 : i * 128 + 128]
        inv = lax.rsqrt(jnp.sum(total, axis=1, keepdims=True) * (1.0 / D) + 1e-06)
        for k in range(D // 512):
            cols = slice(k * 512, k * 512 + 512)
            done = (r.xf[:, cols] * inv * r.gain[0:1, cols]).astype(BF)
            r.xn[at, cols] = done

            @pl.when(fake)
            def _():
                r.xnT[cols, at] = done.T

    steps = {
        0: [(relay_own, 1)], 1: [(relay_near, 0)], 2: [(relay_own, 2), (relay_far, 0)],
        4: [(relay_near, 1)], 5: [(relay_far, 1)], 6: [(relay_near, 2)],
    }
    for i in range(8):
        if i == 2:
            take(NL.at[0 : 3 * 256], r.nx_r)
        embed(mod(X * 2 + i, 8))
        for step, k in steps.get(i, ()):
            step(k)

    def project(half, first, lanes, ks):
        cols = rows(half * HALF, HALF, HALF)
        weight = jnp.concatenate([W[k, cols, :] for k in ks], axis=1)
        for i in range(4):
            at = slice(i * TILE, i * TILE + TILE)
            part = dot(r.xn[at, cols], weight)
            r.qkv[at, lanes] = part if first else r.qkv[at, lanes] + part

    qk_l, v_l = slice(0, 2 * HD), slice(2 * HD, TRIPLE)
    project(c, True, qk_l, (0, 1))
    for k in range(2):
        take(W.at[k, 0 : 6 * PART], r.sb_r.at[k, 0])
        take(W.at[k, 0 : 2 * PART], r.sb_r.at[k, 1])
    project(1 - c, False, qk_l, (0, 1))
    relay_far(2)

    gain_q, gain_k = r.q_gain[0, pl.ds(h, 1), :], r.k_gain[0, pl.ds(h, 1), :]

    def normed(lanes):
        raw = r.qkv[:, lanes]
        inv = lax.rsqrt(jnp.mean(raw * raw, axis=-1, keepdims=True) + 1e-06)
        return raw, inv

    q_l, k_l = slice(0, HD), slice(HD, 2 * HD)
    raw, inv = normed(q_l)
    r.qn[...] = (raw * inv * gain_q).astype(BF)
    raw, inv = normed(k_l)
    k_norm = (raw * inv * gain_k).astype(BF)
    r.kn[...] = k_norm
    r.knT[...] = k_norm.T
    for t in range(4):
        at = slice(t * TILE, t * TILE + TILE)
        scores = dot(r.kn[...], r.qn[at, :], 1, 1)
        expo = jnp.exp2(scores * (SCALE * math.log2(math.e)))
        probs = expo * (1.0 / jnp.sum(expo, axis=0, keepdims=True))
        r.p32[t] = probs
        r.pb[t] = probs.astype(BF)

    project(c, True, v_l, (2,))

    def project_v(dy):
        cols = rows(((1 - c) * NY + mod(y + dy, NY)) * 2 * PART, 2 * PART, 2 * PART)
        for i in range(4):
            at = slice(i * TILE, i * TILE + TILE)
            r.qkv[at, v_l] += dot(r.xn[at, cols], W[2, cols, :])

    take(W.at[2, 0 : 6 * PART], r.sb_r.at[2, 0])
    for dy in (0, 3, 1):
        project_v(dy)
    take(W.at[2, 0 : 2 * PART], r.sb_r.at[2, 1])
    project_v(2)
    value = r.qkv[:, v_l].astype(BF)
    r.v[...] = value
    r.vT[...] = value.T
    loads[2].wait()

    halves = []
    for t in range(4):
        attended = dot(r.vT[...], r.pb[t]).astype(BF)
        halves.append(dot(r.w_outT[...], attended).T)
        if t % 2 == 1:
            x2 = t // 2
            r.pp[x2 * 256 : x2 * 256 + 256, :] = jnp.concatenate(halves, axis=1).astype(BF)
            halves = []
            for dz in FAR_FIRST:
                z2 = mod(z + dz, NZ)
                src, dst = r.pp.at[rows((x2 * NZ + z2) * 32, 32, 32)], r.p1r.at[h]
                if dz:
                    send(src, dst, r.p1_s, r.p1_r, device(g, x2, y, z2, c))
                else:

                    @pl.when(xh == x2)
                    def _():
                        pltpu.make_async_copy(src, dst, r.p1_r).start()

                    @pl.when(xh != x2)
                    def _():
                        send(src, dst, r.p1_s, r.p1_r, device(g, x2, y, z2, c))

    take(r.p1r, r.p1_r)
    pred = jnp.sum(r.p1r[...].astype(F32), axis=0)
    r.pmine[...] = pred

    @pl.when(fake)
    def _():
        lat0 = NL[rows((xh * 2 * NZ + z) * 32, 32, 32), :].astype(F32)[:, CH:]
        lat1 = NL[rows(((xh * 2 + 1) * NZ + z) * 32, 32, 32), :].astype(F32)[:, CH:]
        latent = jnp.concatenate([lat0, lat1], axis=1)
        r.dch[...] = ((pred - latent) * (1.0 / SAMPLES)).astype(BF)
        own = rows(h * 32, 32, 32)
        for dx in (1, 0):
            for dz in FAR_FIRST:
                if dx or dz:
                    target = device(g, mod(xh + dx, XH), y, mod(z + dz, NZ), c)
                    send(r.dch, r.cot.at[own], r.d_s, r.d_r.at[xh], target)
        pltpu.make_async_copy(r.dch, r.cot.at[own], r.d_r.at[xh]).start()

    partner = device(1 - g, xh, y, z, c)
    send(r.pmine, r.pother, r.x_s, r.x_r, partner)

    def generator():
        take(r.pother, r.x_r)
        diff = jnp.where(g == 0, r.pother[...] - r.pmine[...], r.pmine[...] - r.pother[...])
        mine = jnp.where(g == 0, diff[:, 0:CH], diff[:, CH:])
        for j in range(SAMPLES):
            r.gs[j, 0:4, 0:CH] = mine[j * 4 : j * 4 + 4, :]
        for dy in range(NY):
            for dc in range(NC):
                y2, c2 = yc(dy, dc)
                src, dst = r.gs.at[y2 * NC + c2], r.gr.at[me_b]
                if dy or dc:
                    send(src, dst, r.g_s, r.g_r, device(g, xh, y2, z, c2))
                else:
                    pltpu.make_async_copy(src, dst, r.g_r).start()

    def deliver(q, zh, slot, net, x2, head):
        yr, fin, st, R = (getattr(r, name + str(q)) for name in ("yr", "fin", "st", "R"))
        take(yr.at[zh, :, slot], r.y_r.at[q, slot, zh])
        fin[...] = jnp.sum(yr[zh, :, slot].astype(F32), axis=0)
        for i in range(8):
            st[zh, slot, i, 0:12, :] = fin[i * 12 : i * 12 + 12, :].astype(BF)
        fs, fr = r.f_s.at[q], r.f_r.at[q]
        for e in (3, 2, 1, 0):
            zq, zr = mod(z // 4 + e // 2, 2), mod(z + e, 2)
            z2 = zq * 4 + zh * 2 + zr
            for c2 in range(NC):
                src, dst = st.at[zh, slot, (zq * 2 + zr) * NC + c2], R.at[head]
                target = device(net, x2, y, z2, c2)
                if e:
                    send(src, dst, fs, fr, target)
                else:
                    me = (x2 == xh) & (c2 == c) & (z2 == z)

                    @pl.when(me)
                    def _():
                        pltpu.make_async_copy(src, dst, fr).start()

                    @pl.when(jnp.logical_not(me))
                    def _():
                        send(src, dst, fs, fr, target)


    @pl.when(jnp.logical_not(fake))
    def _():
        generator()
        for q in (1, 0):
            for zh in range(2):
                deliver(q, zh, 0, 0, xh, c * NZ + z)
        for q in range(2):
            take(getattr(r, f"R{q}").at[0:15], r.f_s.at[q])

    @pl.when(fake)
    def _():
        def scores_back(i):
            x2 = mod(xh + i // 2, XH)
            if i % 2 == 0:
                take(r.cot.at[0:256], r.d_r.at[x2])
            t = x2 * 2 + i % 2
            at = rows(t * TILE, TILE, TILE)
            cot = r.cot[rows(x2 * 256, 256, 256), (i % 2) * CH : (i % 2) * CH + CH]
            r.d_att[at, :] = dot(cot, r.w_outT[...]).astype(BF)
            d_probs = dot(r.v[...], r.d_att[at, :], 1, 1)
            probs = r.p32[t]
            mean = jnp.sum(probs * d_probs, axis=0, keepdims=True)
            d_score = (probs * (d_probs - mean)).astype(BF)
            dk = dot(d_score, r.qn[at, :])
            if i:
                r.dk[...] += dk
            else:
                r.dk[...] = dk
            r.dq[at, :] = dot(r.knT[...], d_score).T

        def unnorm(lanes, gain, grad):
            raw, inv = normed(lanes)
            scaled = grad * SCALE * gain
            unit = raw * inv
            inner = jnp.mean(unit * scaled, axis=-1, keepdims=True)
            r.dqk[:, lanes] = (inv * (scaled - unit * inner)).astype(BF)

        def place_of(j, x2):
            return (x2 * NY + mod(y + j, NY)) * (PART // 2)

        class Lanes:
            def __init__(self, q, grad):
                self.q, self.grad = q, grad
                for name in ("T", "sibr", "yst", "yr", "R"):
                    setattr(self, name, getattr(r, name + str(q)))

            def block(self, half, zh, js):
                pairs = [(j, x2) for j in js for x2 in range(XH)]
                left = []
                for j, x2 in pairs:
                    first = half * HALF + (x2 * NY + mod(y + j, NY)) * PART + zh * 48
                    left += [r.xnT[rows(first + zq * 96, 48, 48), :] for zq in range(2)]
                out = dot(jnp.concatenate(left, axis=0), self.grad[...]).astype(BF)
                for i, (j, x2) in enumerate(pairs):
                    at = rows(half * (HALF // 2) + place_of(j, x2), 96, 96)
                    self.T[zh, at, :] = out[i * 96 : i * 96 + 96]

            def to_sibling(self, zh, js):
                self.block(1 - c, zh, js)
                for j in js:
                    for x2 in range(XH):
                        src = self.T.at[zh, rows((1 - c) * (HALF // 2) + place_of(j, x2), 96, 96)]
                        dst = self.sibr.at[zh, rows(place_of(j, x2), 96, 96)]
                        send(src, dst, r.ts_s.at[self.q], r.ts_r.at[self.q, j, zh], sib)

            def chunks_out(self, zh, js):
                ys = r.y_s.at[self.q]
                for j in js:
                    take(self.sibr.at[zh, 0:PART], r.ts_r.at[self.q, j, zh])
                    for x2 in range(XH):
                        mine = self.T[zh, rows(c * (HALF // 2) + place_of(j, x2), 96, 96), :]
                        theirs = self.sibr[zh, rows(place_of(j, x2), 96, 96), :]
                        src = self.yst.at[zh, j, x2]
                        src[...] = (mine.astype(F32) + theirs.astype(F32)).astype(BF)

                        @pl.when(c == 0)
                        def _():
                            target = device(0, x2, mod(y + j, NY), z, xh)
                            send(src, self.yr.at[zh, j, 0], ys, r.y_r.at[self.q, 0, zh], target)

                        @pl.when(c == 1)
                        def _():
                            dst, arrive = self.yr.at[zh, j, x2], r.y_r.at[self.q, x2, zh]
                            if j:
                                send(src, dst, ys, arrive, device(1, xh, mod(y + j, NY), z, 1))
                            else:
                                pltpu.make_async_copy(src, dst, arrive).start()

            def drain(self):
                take(self.sibr, r.ts_s.at[self.q])
                take(self.yst.at[:, 0:3], r.y_s.at[self.q])

                @pl.when(c == 0)
                def _():
                    take(self.yst.at[:, 3], r.y_s.at[self.q])

        a, b = Lanes(0, r.dv), Lanes(1, r.dqk)
        near, rest = (2, 1), (3, 0)
        for t in range(4):
            scores_back(t)
        unnorm(q_l, gain_q, r.dq[...])
        unnorm(k_l, gain_k, r.dk[...])
        b.to_sibling(0, near)
        b.to_sibling(0, rest)
        b.block(c, 0, near)
        b.block(c, 0, rest)
        b.chunks_out(0, near)
        b.to_sibling(1, near)
        b.chunks_out(0, rest)
        b.to_sibling(1, rest)
        b.block(c, 1, near)
        b.block(c, 1, rest)
        b.chunks_out(1, near + rest)
        dv = dot(r.pb[0], r.d_att[0:TILE, :])
        for t in range(1, 4):
            dv = dv + dot(r.pb[t], r.d_att[t * TILE : t * TILE + TILE, :])
        r.dv[...] = dv.astype(BF)
        a.to_sibling(0, near)
        a.to_sibling(0, rest)
        a.block(c, 0, near)
        a.block(c, 0, rest)
        a.chunks_out(0, near)
        a.to_sibling(1, near)
        a.to_sibling(1, rest)
        a.chunks_out(0, rest)
        a.block(c, 1, near)
        a.block(c, 1, rest)
        a.chunks_out(1, near + rest)
        generator()

        @pl.when(c == 1)
        def _():
            for q in (1, 0):
                for zh in range(2):
                    for x2 in range(XH):
                        deliver(q, zh, x2, 1, x2, h)
            for R, fs in ((r.R0, r.f_s.at[0]), (r.R1, r.f_s.at[1])):
                take(R, fs)
                take(R.at[0:15], fs)

        a.drain()
        b.drain()
        take(r.cot.at[0 : 15 * 32], r.d_s)

    take(r.n1r.at[0:7], r.n1_s)
    take(r.w0s, r.w0_s)
    take(NL.at[0 : 7 * 32], r.nz_s)
    take(NL.at[0 : 3 * 256], r.nx_s)
    for k in range(3):
        if k == 2:
            left(2)
        take(W.at[k, 0 : 7 * 2 * PART], r.w_s)

    take(r.p1r.at[0:15], r.p1_s)
    take(r.pmine, r.x_s)
    take(r.gr.at[0:7], r.g_s)
    take(r.gr, r.g_r)
    for b in range(SAMPLES):
        r.gen[b * 4 : b * 4 + 4, :] = r.gr[b, 0:4, :]
    take(r.R0, r.f_r.at[0])
    r.Rf[:, :, v_l] = r.R0[...].astype(F32)
    take(r.R1, r.f_r.at[1])
    r.Rf[:, :, qk_l] = r.R1[...].astype(F32)
    for i in range(12):
        r.grad[i * HEADS : i * HEADS + HEADS, :] = r.Rf[:, i, :].astype(BF)


def on_device(latents, noise, steps_t, w_in, norm_gain, w_qkv, q_gain, k_gain, w_out):
    gen, grads = pl.pallas_call(
        mega_kernel,
        out_shape=(
            jax.ShapeDtypeStruct((SAMPLES * 4, 128), F32),
            jax.ShapeDtypeStruct((12 * HEADS, TRIPLE), BF),
        ),
        in_specs=[HB, HB, SM, HB, HB, HB, HB, HB, HB],
        out_specs=(VM, VM),
        scratch_shapes=[pltpu.VMEM(*spec) for spec in SCRATCH.values()]
        + [DMA if n is None else DMA(n if isinstance(n, tuple) else (n,)) for n in SEMS.values()],
        compiler_params=pltpu.CompilerParams(
            collective_id=0, has_side_effects=True, vmem_limit_bytes=58 * 1024 * 1024
        ),
        name="distill_step",
    )(latents, noise, steps_t, w_in, norm_gain, w_qkv, q_gain, k_gain, w_out.transpose(0, 2, 1))
    grads = grads.astype(F32).reshape(12, HEADS, TRIPLE).transpose(1, 0, 2)
    return gen[:, :CH].reshape(SAMPLES, 4, CH), grads


def solution(mesh):
    return jax.shard_map(
        on_device,
        mesh=mesh,
        in_specs=(
            P(None, ("grp", "mp"), None),
            P(None, ("grp", "mp"), None),
            P(),
            P("grp", None, None),
            P("grp", None),
            P("grp", None, "mp", None),
            P("grp", None, None),
            P("grp", None, None),
            P("grp", None, None),
        ),
        out_specs=(P(None, ("grp", "mp"), None), P(None, ("grp", "mp"), None)),
        check_vma=False,
    )
```
